256 devices in a mesh: seq: 256 (over z, y, x, core).
Axes of the slice: x: 4, y: 4, z: 8, core: 2. Of those that a mesh axis runs over, the one named last changes fastest.
Arguments:
- query_rows: bfloat16 [65536, 768], P('seq'), may hold values from -12 to 12
- key_rows: bfloat16 [65536, 768], P('seq'), may hold values from -12 to 12
- value_rows: bfloat16 [65536, 768], P('seq'), may hold values from -6 to 6
- grad_out: bfloat16 [65536, 768], P('seq'), may hold values from -6 to 6
- head_offset: int32 [3, 12], replicated, may hold values from 0 to 255, as said below
Outputs:
- attended: bfloat16 [65536, 768], P('seq')
- grad_query: bfloat16 [65536, 768], P('seq')
- grad_key: bfloat16 [65536, 768], P('seq')
- grad_value: bfloat16 [65536, 768], P('seq')
The draws below stay inside these ranges and needn't reach their ends.
Inputs may be any that keep to these rules, and one draw needn't show every extreme that they name: `head_offset`: row l holds offsets from 0 to g * 1 - 1, with g = 4, 16, 256 for l = 0, 1, 2.
All inputs are finite; a program needn't handle non-finite values.
Results may differ from the reference program's by a relative error of at most 0.022.
Values may be sent and summed in bfloat16 or wider, within the bound.
A program may use at most 128 MiB of HBM per device.

```python
import jax
import jax.numpy as jnp
from jax import lax

HEADS = 12
HEAD_DIM = 64
D = 768
TILE = 64
TILES_DEV = 4
TOKENS = 65536
GROUP_A = 4
GROUP_B = 16
N_SEQ = 256


def draw_query_rows(key, part):
    key = jax.random.fold_in(key, 1)
    return jnp.clip(jax.random.normal(key, (TOKENS, D), jnp.float32), -12.0, 12.0).astype(jnp.bfloat16)


def draw_key_rows(key, part):
    key = jax.random.fold_in(key, 2)
    return jnp.clip(jax.random.normal(key, (TOKENS, D), jnp.float32), -12.0, 12.0).astype(jnp.bfloat16)


def draw_head_offset(key, part):
    key = jax.random.fold_in(key, 5)
    limits = (GROUP_A * TILES_DEV // 4, GROUP_B * TILES_DEV // 4, N_SEQ * TILES_DEV // 4)
    offset_rows = []
    for number, upper_limit in enumerate(limits):
        level_key = jax.random.fold_in(key, number)
        offset_draws = jax.random.randint(level_key, (HEADS,), 0, upper_limit)
        chosen_head = jax.random.randint(jax.random.fold_in(level_key, 50), (), 0, HEADS)
        forced = 0 if number == 0 else upper_limit - 1
        offset_draws = jnp.where(jnp.arange(HEADS) == chosen_head, forced, offset_draws)
        offset_rows.append(offset_draws)
    return jnp.stack(offset_rows).astype(jnp.int32)


def level_of(rng, dims, split, smallest, largest):
    def one(axis_at, blocks):
        heights = jax.random.uniform(jax.random.fold_in(jax.random.fold_in(rng, 6), axis_at), (blocks,), jnp.float32, smallest / len(split), largest / len(split))
        return jnp.repeat(jnp.exp(heights), dims[axis_at] // blocks).reshape((-1,) + (1,) * (len(dims) - axis_at - 1))

    factor_of = one(*split[0])
    for cut in split[1:]:
        factor_of = factor_of * one(*cut)
    return factor_of


def centred(key, dims, width, reach, split=(), kind=jnp.bfloat16):
    gain = level_of(key, dims, split, -0.22, 0.18) if split else 1.0
    result = jax.random.normal(key, dims, jnp.float32) * width * gain
    return jnp.minimum(jnp.maximum(result, -reach), reach).astype(kind)


def setup_inputs(seed: int = 0) -> dict:
    streams_of = jax.random.split(jax.random.key(seed), 6)
    return {
        "query_rows": draw_query_rows(jax.random.fold_in(streams_of[5], 71), 0),
        "key_rows": draw_key_rows(jax.random.fold_in(streams_of[5], 71), 0),
        "value_rows": centred(streams_of[2], (TOKENS, D), 1.0, 6.0, ((0, 256),)),
        "grad_out": centred(streams_of[3], (TOKENS, D), 1.0, 6.0, ((0, 256),)),
        "head_offset": draw_head_offset(jax.random.fold_in(streams_of[5], 71), 0),
    }


NEG_FILL = -1.0e30


def round_trip(values):
    return lax.optimization_barrier(values.astype(jnp.bfloat16)).astype(jnp.float32)


def dilated_tiles(offset, group_size):
    segment = group_size * TILES_DEV
    stride = segment // 4
    seg_count = N_SEQ // group_size
    starts = jnp.arange(seg_count, dtype=jnp.int32) * segment
    steps_along = jnp.arange(4, dtype=jnp.int32) * stride
    return (starts[:, None] + offset.astype(jnp.int32) + steps_along[None, :]).astype(jnp.int32)


def pick_block(head_rows, tile_index):
    seg_count, seg_width = tile_index.shape
    return head_rows[tile_index].reshape(seg_count, seg_width * TILE, HEAD_DIM).astype(jnp.float32)


def level_forward(query_head, key_head, value_head, tile_index):
    seg_count, seg_width = tile_index.shape
    query_block = pick_block(query_head, tile_index)
    key_block = pick_block(key_head, tile_index)
    value_block = pick_block(value_head, tile_index)
    scores = jnp.einsum("sqd,skd->sqk", query_block, key_block) * HEAD_DIM ** -0.5
    row_peak = jnp.max(scores, axis=-1)
    exponent = jnp.exp(scores - row_peak[:, :, None])
    row_total = jnp.sum(exponent, axis=-1)
    numer = jnp.einsum("sqk,skd->sqd", round_trip(exponent), value_block)
    tiles_all = N_SEQ * TILES_DEV
    peak_full = jnp.full((tiles_all, TILE), NEG_FILL, jnp.float32)
    peak_full = peak_full.at[tile_index].set(row_peak.reshape(seg_count, seg_width, TILE))
    total_full = jnp.zeros((tiles_all, TILE), jnp.float32)
    total_full = total_full.at[tile_index].set(row_total.reshape(seg_count, seg_width, TILE))
    numer_full = jnp.zeros((tiles_all, TILE, HEAD_DIM), jnp.float32)
    numer_full = numer_full.at[tile_index].set(numer.reshape(seg_count, seg_width, TILE, HEAD_DIM))
    return peak_full, total_full, numer_full


def level_backward(query_head, key_head, value_head, grad_head, log_total, row_delta, tile_index):
    seg_count, seg_width = tile_index.shape
    span = seg_width * TILE
    query_block = pick_block(query_head, tile_index)
    key_block = pick_block(key_head, tile_index)
    value_block = pick_block(value_head, tile_index)
    grad_block = pick_block(grad_head, tile_index)
    lse_block = log_total[tile_index].reshape(seg_count, span)
    delta_block = row_delta[tile_index].reshape(seg_count, span)
    scores = jnp.einsum("sqd,skd->sqk", query_block, key_block) * HEAD_DIM ** -0.5
    pair_prob = jnp.exp(scores - lse_block[:, :, None])
    grad_value = jnp.einsum("sqk,sqd->skd", round_trip(pair_prob), grad_block)
    grad_inner = jnp.einsum("sqd,skd->sqk", grad_block, value_block)
    grad_scores = round_trip(pair_prob * (grad_inner - delta_block[:, :, None]) * HEAD_DIM ** -0.5)
    grad_query = jnp.einsum("sqk,skd->sqd", grad_scores, key_block)
    grad_key = jnp.einsum("sqk,sqd->skd", grad_scores, query_block)
    zero_rows = jnp.zeros((N_SEQ * TILES_DEV, TILE, HEAD_DIM), jnp.float32)
    shaped = (seg_count, seg_width, TILE, HEAD_DIM)
    return (zero_rows.at[tile_index].add(grad_query.reshape(shaped)),
            zero_rows.at[tile_index].add(grad_key.reshape(shaped)),
            zero_rows.at[tile_index].add(grad_value.reshape(shaped)))


def head_pass(inputs):
    query_head, key_head, value_head, grad_head, offsets = inputs
    tiles_all = N_SEQ * TILES_DEV
    tile_sets = [jnp.arange(tiles_all, dtype=jnp.int32).reshape(N_SEQ, TILES_DEV)]
    for number, group_size in enumerate((GROUP_A, GROUP_B, N_SEQ)):
        tile_sets.append(dilated_tiles(offsets[number], group_size))
    forward_parts = [level_forward(query_head, key_head, value_head, tile_index) for tile_index in tile_sets]
    row_top = forward_parts[0][0]
    for part in forward_parts[1:]:
        row_top = jnp.maximum(row_top, part[0])
    total = jnp.zeros((tiles_all, TILE), jnp.float32)
    numer_sum = jnp.zeros((tiles_all, TILE, HEAD_DIM), jnp.float32)
    for part in forward_parts:
        factor = jnp.exp(part[0] - row_top)
        total = total + part[1] * factor
        numer_sum = numer_sum + part[2] * factor[:, :, None]
    attended = (numer_sum / total[:, :, None]).astype(jnp.bfloat16)
    log_total = row_top + jnp.log(total)
    row_delta = jnp.sum(grad_head.astype(jnp.float32) * attended.astype(jnp.float32), axis=-1)
    grad_query = jnp.zeros((tiles_all, TILE, HEAD_DIM), jnp.float32)
    grad_key = jnp.zeros((tiles_all, TILE, HEAD_DIM), jnp.float32)
    grad_value = jnp.zeros((tiles_all, TILE, HEAD_DIM), jnp.float32)
    for tile_index in tile_sets:
        parts = level_backward(query_head, key_head, value_head, grad_head, log_total, row_delta, tile_index)
        grad_query = grad_query + parts[0]
        grad_key = grad_key + parts[1]
        grad_value = grad_value + parts[2]
    return (attended, grad_query.astype(jnp.bfloat16), grad_key.astype(jnp.bfloat16), grad_value.astype(jnp.bfloat16))


def reference(query_rows, key_rows, value_rows, grad_out, head_offset):
    tiles_all = N_SEQ * TILES_DEV

    def by_head(rows):
        return rows.reshape(tiles_all, TILE, HEADS, HEAD_DIM).transpose(2, 0, 1, 3)

    def by_row(block):
        return block.transpose(1, 2, 0, 3).reshape(TOKENS, HEADS * HEAD_DIM)

    results = lax.map(head_pass, (by_head(query_rows), by_head(key_rows), by_head(value_rows), by_head(grad_out), head_offset.T))
    return (by_row(results[0]), by_row(results[1]), by_row(results[2]), by_row(results[3]))
```

```python
import jax
import jax.numpy as jnp
from jax import lax
from jax.experimental import pallas as pl
from jax.experimental.pallas import tpu as pltpu
from jax.sharding import PartitionSpec as P

HEADS = 12
HEAD_DIM = 64
TILE = 64
PAIRS = 3
HALF = 384
ROWS = 256
SCALE = HEAD_DIM**-0.5
SCALE2 = SCALE * 1.4426950408889634
FAR = 1e30
MESH = pl.DeviceIdType.MESH
SIB = 1
MASK_A = (2,)
MASK_B = (4, 8, 12)
MASK_C = (64, 128, 192)
F32 = jnp.float32
BF16 = jnp.bfloat16


def dot_nt(a, b):
    return lax.dot_general(a, b, (((1,), (1,)), ((), ())), preferred_element_type=F32)


def dot_nn(a, b):
    return lax.dot_general(a, b, (((1,), (0,)), ((), ())), preferred_element_type=F32)


def dot_tn(a, b):
    return lax.dot_general(a, b, (((0,), (0,)), ((), ())), preferred_element_type=F32)


def low_lanes(rows):
    return lax.broadcasted_iota(jnp.int32, (rows, 128), 1) < 64


def cat2(x):
    low = low_lanes(x.shape[0])
    zero = jnp.zeros_like(x)
    return jnp.concatenate([jnp.where(low, x, zero), jnp.where(low, zero, x)], axis=0)


def sel2(y):
    n = y.shape[0] // 2
    return jnp.where(low_lanes(n), y[:n], y[n:])


def stats_of(kk, vv, qc, gc):
    s = dot_nt(kk, qc) * SCALE2
    m = jnp.max(s, axis=0, keepdims=True)
    p = jnp.exp2(s - m)
    tot = jnp.sum(p, axis=0, keepdims=True)
    d = jnp.sum(p * dot_nt(vv, gc), axis=0, keepdims=True)
    return m, tot, d


def probs_of(kk, vv, qc, gc, lrow, drow):
    p = jnp.exp2(dot_nt(kk, qc) * SCALE2 - lrow)
    ds = (p * (dot_nt(vv, gc) - drow) * SCALE).astype(BF16)
    return p.astype(BF16), ds


def kernel(
    off, q_hbm, k_hbm, v_hbm, g_hbm,
    o_att, o_dq, o_dk, o_dv,
    xq, xk, xv, xg, ha, hb, hc, acc, stage, ca, cb, cc,
    lst, sta, stb, stc, ls, ea, eb, ec,
    in_sem, s1_send, s1_recv, x1_send, x1_recv, x2_send, x2_recv, out_sem, o_send, o_recv,
):
    me = lax.axis_index("seq")
    core = lax.rem(me, 2)
    other = 1 - core
    chip = me // 2
    masks = (SIB,) + MASK_A + MASK_B + MASK_C
    barrier = pltpu.get_barrier_semaphore()
    for m in masks:
        pl.semaphore_signal(barrier, inc=1, device_id=(me ^ m,), device_id_type=MESH)

    my_cols = pl.ds(pl.multiple_of(core * HALF, 128), HALF)
    sib_cols = pl.ds(pl.multiple_of(other * HALF, 128), HALF)
    my_rows = pl.ds(pl.multiple_of(core * ROWS, ROWS), ROWS)
    sib_rows = pl.ds(pl.multiple_of(other * ROWS, ROWS), ROWS)
    hbm = (k_hbm, v_hbm, q_hbm, g_hbm)
    xs = (xk, xv, xq, xg)
    loads = [
        pltpu.make_async_copy(h.at[:, my_cols], x.at[my_rows, :], in_sem.at[i])
        for i, (h, x) in enumerate(zip(hbm, xs))
    ]
    for c in loads:
        c.start()

    def head(level, j):
        return off[level, core * 6 + j]

    def live_b(j):
        o = head(1, j)
        return jnp.where(lax.rem(chip, 2) == o // 8, lax.rem(o, 8), -1)

    def live_c(j):
        o = head(2, j)
        return jnp.where(lax.rem(chip, 32) == o // 8, lax.rem(o, 8), -1)

    def local_stats(seg):
        rows = pl.ds(pl.multiple_of(seg * ROWS, ROWS), ROWS)

        def body(p, carry):
            cols = pl.ds(pl.multiple_of(p * 128, 128), 128)
            out = stats_of(xk[rows, cols], xv[rows, cols], cat2(xq[rows, cols]), cat2(xg[rows, cols]))
            for n, x in enumerate(out):
                for i in range(2):
                    lst[n, seg, pl.ds(2 * p + i, 1), :] = x[:, i * ROWS : (i + 1) * ROWS]
            return carry

        lax.fori_loop(0, PAIRS, body, 0)

    zero8 = jnp.zeros((8, ROWS), F32)
    for n in range(3):
        for s in range(2):
            lst[n, s] = zero8
        for st in (sta, stb, stc):
            st[n] = zero8[:, :128]

    for c in loads:
        c.wait()
    local_stats(core)
    pl.semaphore_wait(barrier, len(masks))

    def remote(src, dst, send, recv, mask):
        return pltpu.make_async_remote_copy(
            src_ref=src, dst_ref=dst, send_sem=send, recv_sem=recv,
            device_id=(me ^ mask,), device_id_type=MESH,
        )

    s1 = [
        remote(h.at[:, sib_cols], x.at[my_rows, :], s1_send.at[i], s1_recv.at[i], SIB)
        for i, (h, x) in enumerate(zip(hbm, xs))
    ]
    for c in s1:
        c.start()

    def pick(first):
        def body(p, carry):
            cols = pl.ds(pl.multiple_of(p * 128, 128), 128)
            low = lax.broadcasted_iota(jnp.int32, (1, 128), 1) < 64
            want_a = jnp.where(low, head(0, 2 * p), head(0, 2 * p + 1))
            want_b = jnp.where(low, lax.rem(head(1, 2 * p), 8), lax.rem(head(1, 2 * p + 1), 8))
            want_c = jnp.where(low, lax.rem(head(2, 2 * p), 8), lax.rem(head(2, 2 * p + 1), 8))

            def ones(want, count):
                return [jnp.where(want == t, 1.0, 0.0).astype(BF16) for t in range(count)]

            hot_a, hot_b, hot_c = ones(want_a, 4), ones(want_b, 8), ones(want_c, 8)

            def mix(tiles, hot):
                out = tiles[0] * hot[0]
                for tile, one in zip(tiles[1:], hot[1:]):
                    out += tile * one
                return out

            for n in (first, first + 1):
                tiles = [xs[n][pl.ds(t * TILE, TILE), cols] for t in range(8)]
                hc[n, 0, :, cols] = mix(tiles, hot_c)
                hb[n, 0, :, cols] = mix(tiles, hot_b)
                for s in range(2):
                    ha[n, s, :, cols] = mix(tiles[4 * s : 4 * s + 4], hot_a)
            return carry

        lax.fori_loop(0, PAIRS, body, 0)

    def send_tiles(half):
        two = pl.ds(2 * half, 2)
        base = 7 * half
        copies = []
        for i, m in enumerate(MASK_C):
            copies.append(remote(hc.at[two, 0], hc.at[two, i + 1], x1_send.at[base + i], x1_recv.at[base + i], m))
        for i, m in enumerate(MASK_B):
            copies.append(remote(hb.at[two, 0], hb.at[two, i + 1], x1_send.at[base + 3 + i], x1_recv.at[base + 3 + i], m))
        copies.append(
            remote(ha.at[two, pl.ds(0, 2)], ha.at[two, pl.ds(2, 2)], x1_send.at[base + 6], x1_recv.at[base + 6], MASK_A[0])
        )
        for c in copies:
            c.start()
        return copies

    s1[0].wait()
    s1[1].wait()
    pick(0)
    kv_copies = send_tiles(0)
    s1[2].wait()
    s1[3].wait()
    pick(2)
    qg_copies = send_tiles(1)
    local_stats(other)

    levels = ((ha, 2, sta, ca), (hb, 1, stb, cb), (hc, 1, stc, cc))

    def all_rows(h, n, cols):
        return h[n, :, :, cols].reshape(4 * TILE, 128)

    def own_rows(h, n, slots, cols):
        return h[n, pl.ds(0, slots), :, cols].reshape(slots * TILE, 128)

    def level_stats(h, slots, st):
        width = slots * TILE

        def body(p, carry):
            cols = pl.ds(pl.multiple_of(p * 128, 128), 128)
            out = stats_of(
                all_rows(h, 0, cols), all_rows(h, 1, cols),
                cat2(own_rows(h, 2, slots, cols)), cat2(own_rows(h, 3, slots, cols)),
            )
            for n, x in enumerate(out):
                for i in range(2):
                    st[n, pl.ds(2 * p + i, 1), pl.ds(0, width)] = x[:, i * width : (i + 1) * width]
            return carry

        lax.fori_loop(0, PAIRS, body, 0)

    kv_copies[6].wait()
    level_stats(ha, 2, sta)
    for c in kv_copies[3:6]:
        c.wait()
    level_stats(hb, 1, stb)
    for c in kv_copies[:3]:
        c.wait()
    level_stats(hc, 1, stc)

    row_id = lax.broadcasted_iota(jnp.int32, (8, ROWS), 0)
    lane_tile = lax.broadcasted_iota(jnp.int32, (8, ROWS), 1) // TILE

    def per_head(f, fill):
        out = jnp.full((8, ROWS), fill, jnp.int32)
        for j in range(6):
            out = jnp.where(row_id == j, f(j), out)
        return out

    tile_a = per_head(lambda j: head(0, j), 0)
    tile_b = per_head(live_b, -1)
    tile_c = per_head(live_c, -1)

    def rep4(x):
        return jnp.concatenate([x] * 4, axis=1)

    lse, delta = [], []
    for s in range(2):
        hits = (lane_tile == tile_a, lane_tile + 4 * s == tile_b, lane_tile + 4 * s == tile_c)
        parts = [tuple(lst[n, s] for n in range(3))]
        for hit, st, start in zip(hits, (sta, stb, stc), (s * TILE, 0, 0)):
            peak, tot, d = (rep4(st[n, :, pl.ds(start, TILE)]) for n in range(3))
            parts.append((jnp.where(hit, peak, -FAR), jnp.where(hit, tot, 0.0), jnp.where(hit, d, 0.0)))
        top = parts[0][0]
        for part in parts[1:]:
            top = jnp.maximum(top, part[0])
        total = jnp.zeros((8, ROWS), F32)
        dsum = jnp.zeros((8, ROWS), F32)
        for peak, tot, d in parts:
            factor = jnp.exp2(peak - top)
            total += tot * factor
            dsum += d * factor
        lse.append(top + jnp.log2(total))
        delta.append(dsum / total)
        ls[s, pl.ds(0, 8), :] = lse[s]
        ls[s, pl.ds(8, 8), :] = delta[s]

    def gather8(values, index, tiles):
        out = jnp.zeros((8, TILE), F32)
        for t in tiles:
            out = jnp.where(index[:, :TILE] == t % 8, values[t // 4 % 2][:, t % 4 * TILE : (t % 4 + 1) * TILE], out)
        return out

    for base, values in ((0, lse), (8, delta)):
        halves = []
        for s in range(2):
            out = jnp.zeros((8, TILE), F32)
            for t in range(4):
                out = jnp.where(tile_a[:, :TILE] == t, values[s][:, t * TILE : (t + 1) * TILE], out)
            halves.append(out)
        ea[0, pl.ds(base, 8), :] = jnp.concatenate(halves, axis=1)
        for e, index in ((eb, tile_b), (ec, tile_c)):
            out = gather8(values, index, range(8))
            if base == 0:
                out = jnp.where(index[:, :TILE] < 0, FAR, out)
            e[0, pl.ds(base, 8), :] = jnp.concatenate([out, out], axis=1)

    x2 = []
    for i, m in enumerate(MASK_C):
        x2.append(remote(ec.at[0], ec.at[i + 1], x2_send.at[i], x2_recv.at[i], m))
    for i, m in enumerate(MASK_B):
        x2.append(remote(eb.at[0], eb.at[i + 1], x2_send.at[3 + i], x2_recv.at[3 + i], m))
    x2.append(remote(ea.at[0], ea.at[1], x2_send.at[6], x2_recv.at[6], MASK_A[0]))
    for c in x2:
        c.start()

    low_row = lax.broadcasted_iota(jnp.int32, (1, 128), 1) < 64

    def local_back(n, carry):
        seg, p = n // PAIRS, lax.rem(n, PAIRS)
        rows = pl.ds(pl.multiple_of(seg * ROWS, ROWS), ROWS)
        cols = pl.ds(pl.multiple_of(p * 128, 128), 128)
        kk, vv = xk[rows, cols], xv[rows, cols]
        qc, gc = cat2(xq[rows, cols]), cat2(xg[rows, cols])
        lrow = jnp.concatenate([ls[seg, pl.ds(2 * p + i, 1), :] for i in range(2)], axis=1)
        drow = jnp.concatenate([ls[seg, pl.ds(8 + 2 * p + i, 1), :] for i in range(2)], axis=1)
        pb, ds = probs_of(kk, vv, qc, gc, lrow, drow)
        acc[0, rows, cols] = sel2(dot_tn(pb, vv))
        acc[1, rows, cols] = sel2(dot_tn(ds, kk))
        acc[2, rows, cols] = dot_nn(ds, qc)
        acc[3, rows, cols] = dot_nn(pb, gc)
        return carry

    lax.fori_loop(0, 2 * PAIRS, local_back, 0)

    def level_query(h, slots, e, c):
        def body(p, carry):
            cols = pl.ds(pl.multiple_of(p * 128, 128), 128)
            kk, vv = all_rows(h, 0, cols), all_rows(h, 1, cols)
            qc, gc = cat2(own_rows(h, 2, slots, cols)), cat2(own_rows(h, 3, slots, cols))
            rows = []
            for base in (0, 8):
                r0, r1 = (e[0, pl.ds(base + 2 * p + i, 1), :] for i in range(2))
                rows.append(jnp.concatenate([r0, r1], axis=1) if slots == 2 else jnp.where(low_row, r0, r1))
            pb, ds = probs_of(kk, vv, qc, gc, *rows)
            c[0, :, cols] = sel2(dot_tn(pb, vv))
            c[1, :, cols] = sel2(dot_tn(ds, kk))
            return carry

        lax.fori_loop(0, PAIRS, body, 0)

    def level_key(h, slots, e, c):
        n = slots * TILE

        def body(p, carry):
            cols = pl.ds(pl.multiple_of(p * 128, 128), 128)
            qq, gg = all_rows(h, 2, cols), all_rows(h, 3, cols)
            kc, vc = cat2(own_rows(h, 0, slots, cols)), cat2(own_rows(h, 1, slots, cols))

            def stat_row(r):
                if slots == 2:
                    return jnp.concatenate([e[0, pl.ds(r, 1), :], e[1, pl.ds(r, 1), :]], axis=1)
                s = [e[i, pl.ds(r, 1), :] for i in range(4)]
                return jnp.concatenate([jnp.where(low_row, s[0], s[1]), jnp.where(low_row, s[2], s[3])], axis=1)

            sc = dot_nt(kc, qq) * SCALE2
            dp = dot_nt(vc, gg)
            pbs, dss = [], []
            for i in range(2):
                part = slice(i * n, (i + 1) * n)
                pr = jnp.exp2(sc[part] - stat_row(2 * p + i))
                dss.append((pr * (dp[part] - stat_row(8 + 2 * p + i)) * SCALE).astype(BF16))
                pbs.append(pr.astype(BF16))
            c[2, :, cols] = sel2(dot_nn(jnp.concatenate(dss, axis=0), qq))
            c[3, :, cols] = sel2(dot_nn(jnp.concatenate(pbs, axis=0), gg))
            return carry

        lax.fori_loop(0, PAIRS, body, 0)

    def finish(outs):
        def body(p, carry):
            cols = pl.ds(pl.multiple_of(p * 128, 128), 128)
            low = low_lanes(TILE)
            pick_a = jnp.where(low, head(0, 2 * p), head(0, 2 * p + 1))
            pick_b = jnp.where(low, live_b(2 * p), live_b(2 * p + 1))
            pick_c = jnp.where(low, live_c(2 * p), live_c(2 * p + 1))
            for o in outs:
                b, c = cb[o, :, cols], cc[o, :, cols]
                for t in range(8):
                    rows = pl.ds(t * TILE, TILE)
                    a = ca[o, pl.ds(t // 4 * TILE, TILE), cols]
                    total = acc[o, rows, cols] + jnp.where(pick_a == t % 4, a, 0.0)
                    total += jnp.where(pick_b == t, b, 0.0)
                    total += jnp.where(pick_c == t, c, 0.0)
                    stage[o, rows, cols] = total.astype(BF16)
            return carry

        lax.fori_loop(0, PAIRS, body, 0)

    o_refs = (o_att, o_dq, o_dk, o_dv)

    def put(outs):
        copies = []
        for o in outs:
            copies.append(remote(stage.at[o, sib_rows, :], o_refs[o].at[:, my_cols], o_send.at[o], o_recv.at[o], SIB))
        for o in outs:
            copies.append(pltpu.make_async_copy(stage.at[o, my_rows, :], o_refs[o].at[:, my_cols], out_sem.at[o]))
        for c in copies:
            c.start()
        return copies

    es = (ea, eb, ec)
    for (h, slots, _, c), e in zip(levels, es):
        level_query(h, slots, e, c)
    finish((0, 1))
    final = put((0, 1))
    waits = ((6, 7), (3, 6), (0, 3))
    for (h, slots, _, c), e, (lo, hi) in zip(levels, es, waits):
        for i in range(lo, hi):
            qg_copies[i].wait()
            x2[i].wait()
        level_key(h, slots, e, c)
    finish((2, 3))
    final += put((2, 3))
    for c in final:
        c.wait()


def local(query_rows, key_rows, value_rows, grad_out, head_offset):
    rows = jax.ShapeDtypeStruct((ROWS, 2 * HALF), BF16)
    any_spec = pl.BlockSpec(memory_space=pl.ANY)
    dma = pltpu.SemaphoreType.DMA
    tile4 = pltpu.VMEM((4, 4, TILE, HALF), BF16)
    return pl.pallas_call(
        kernel,
        out_shape=[rows] * 4,
        in_specs=[pl.BlockSpec(memory_space=pltpu.SMEM)] + [any_spec] * 4,
        out_specs=[any_spec] * 4,
        scratch_shapes=[pltpu.VMEM((2 * ROWS, HALF), BF16)] * 4
        + [tile4] * 3
        + [
            pltpu.VMEM((4, 2 * ROWS, HALF), F32),
            pltpu.VMEM((4, 2 * ROWS, HALF), BF16),
            pltpu.VMEM((4, 2 * TILE, HALF), F32),
            pltpu.VMEM((4, TILE, HALF), F32),
            pltpu.VMEM((4, TILE, HALF), F32),
            pltpu.VMEM((3, 2, 8, ROWS), F32),
            pltpu.VMEM((3, 8, 128), F32),
            pltpu.VMEM((3, 8, 128), F32),
            pltpu.VMEM((3, 8, 128), F32),
            pltpu.VMEM((2, 16, ROWS), F32),
            pltpu.VMEM((2, 16, 128), F32),
            pltpu.VMEM((4, 16, 128), F32),
            pltpu.VMEM((4, 16, 128), F32),
            dma((4,)), dma((4,)), dma((4,)), dma((14,)), dma((14,)), dma((7,)), dma((7,)), dma((4,)), dma((4,)), dma((4,)),
        ],
        compiler_params=pltpu.CompilerParams(
            collective_id=0, has_side_effects=True, vmem_limit_bytes=40 * 1024 * 1024
        ),
        cost_estimate=pl.CostEstimate(flops=2_000_000_000, bytes_accessed=3_200_000, transcendentals=3_000_000),
    )(head_offset, query_rows, key_rows, value_rows, grad_out)


def solution(mesh):
    return jax.shard_map(
        local,
        mesh=mesh,
        in_specs=(P("seq", None), P("seq", None), P("seq", None), P("seq", None), P()),
        out_specs=(P("seq", None), P("seq", None), P("seq", None), P("seq", None)),
        check_vma=False,
    )
```

```python
import jax
import jax.numpy as jnp
from jax import lax
from jax.experimental import pallas as pl
from jax.experimental.pallas import tpu as pltpu
from jax.sharding import PartitionSpec as P

HEADS = 12
HEAD_DIM = 64
TILE = 64
PAIRS = 3
HALF = 384
ROWS = 256
SCALE = HEAD_DIM**-0.5
SCALE2 = SCALE * 1.4426950408889634
FAR = 1e30
MESH = pl.DeviceIdType.MESH
SIB = 1
MASK_A = (2,)
MASK_B = (4, 8, 12)
MASK_C = (64, 128, 192)
F32 = jnp.float32
BF16 = jnp.bfloat16


def dot_nt(a, b):
    return lax.dot_general(a, b, (((1,), (1,)), ((), ())), preferred_element_type=F32)


def dot_nn(a, b):
    return lax.dot_general(a, b, (((1,), (0,)), ((), ())), preferred_element_type=F32)


def dot_tn(a, b):
    return lax.dot_general(a, b, (((0,), (0,)), ((), ())), preferred_element_type=F32)


def low_lanes(rows):
    return lax.broadcasted_iota(jnp.int32, (rows, 128), 1) < 64


def cat2(x):
    low = low_lanes(x.shape[0])
    zero = jnp.zeros_like(x)
    return jnp.concatenate([jnp.where(low, x, zero), jnp.where(low, zero, x)], axis=0)


def sel2(y):
    n = y.shape[0] // 2
    return jnp.where(low_lanes(n), y[:n], y[n:])


def stats_of(kk, vv, qc, gc):
    s = dot_nt(kk, qc) * SCALE2
    m = jnp.max(s, axis=0, keepdims=True)
    p = jnp.exp2(s - m)
    tot = jnp.sum(p, axis=0, keepdims=True)
    dp = dot_nt(vv, gc)
    d = jnp.sum(p * dp, axis=0, keepdims=True)
    return (m, tot, d), p, dp


def probs_of(p, dp, peak, lrow, drow):
    p = p * jnp.exp2(peak - lrow)
    return p.astype(BF16), (p * SCALE * (dp - drow)).astype(BF16)


def dup_lanes(x, upper):
    low = low_lanes(x.shape[0])
    other = pltpu.roll(x, 64, 1)
    return jnp.where(low, other, x) if upper else jnp.where(low, x, other)


def kernel(
    off_hbm, q_hbm, k_hbm, v_hbm, g_hbm,
    o_att, o_dq, o_dk, o_dv,
    xq, xk, xv, xg, xkt, xvt, ha, hb, hc, acc, acct, stage, ca, cb, cc, cat, cbt, cct,
    lp, ldp, ap, adp, bp, bdp, cp, cdp,
    lst, sta, stb, stc, ls, ea, eb, ec,
    off, off_sem, in_sem, s1_send, s1_recv, x1_send, x1_recv, x2_send, x2_recv, out_sem, o_send, o_recv,
):
    me = lax.axis_index("seq")
    core = lax.rem(me, 2)
    other = 1 - core
    chip = me // 2
    masks = (SIB,) + MASK_A + MASK_B + MASK_C
    barrier = pltpu.get_barrier_semaphore()
    for m in masks:
        pl.semaphore_signal(barrier, inc=1, device_id=(me ^ m,), device_id_type=MESH)

    my_cols = pl.ds(pl.multiple_of(core * HALF, 128), HALF)
    sib_cols = pl.ds(pl.multiple_of(other * HALF, 128), HALF)
    my_rows = pl.ds(pl.multiple_of(core * ROWS, ROWS), ROWS)
    sib_rows = pl.ds(pl.multiple_of(other * ROWS, ROWS), ROWS)
    hbm = (k_hbm, v_hbm, q_hbm, g_hbm)
    xs = (xk, xv, xq, xg)
    loads = [
        pltpu.make_async_copy(h.at[:, my_cols], x.at[my_rows, :], in_sem.at[i])
        for i, (h, x) in enumerate(zip(hbm, xs))
    ]
    load_off = pltpu.make_async_copy(off_hbm, off, off_sem)
    for c in loads:
        c.start()
    load_off.start()

    def head(level, j):
        return off[level, core * 6 + j]

    def live_b(j):
        o = head(1, j)
        return jnp.where(lax.rem(chip, 2) == o // 8, lax.rem(o, 8), -1)

    def live_c(j):
        o = head(2, j)
        return jnp.where(lax.rem(chip, 32) == o // 8, lax.rem(o, 8), -1)

    def local_stats(seg):
        rows = pl.ds(pl.multiple_of(seg * ROWS, ROWS), ROWS)

        def body(p, carry):
            cols = pl.ds(pl.multiple_of(p * 128, 128), 128)
            kk, vv = xk[rows, cols], xv[rows, cols]
            out, lp[seg, p], ldp[seg, p] = stats_of(kk, vv, cat2(xq[rows, cols]), cat2(xg[rows, cols]))
            xkt[seg, cols, :] = kk.T
            xvt[seg, cols, :] = vv.T
            for n, x in enumerate(out):
                for i in range(2):
                    lst[n, seg, pl.ds(2 * p + i, 1), :] = x[:, i * ROWS : (i + 1) * ROWS]
            return carry

        lax.fori_loop(0, PAIRS, body, 0, unroll=True)

    zero8 = jnp.zeros((8, ROWS), F32)
    for n in range(3):
        for s in range(2):
            lst[n, s] = zero8
        for st in (sta, stb, stc):
            st[n] = zero8[:, :128]

    for c in loads:
        c.wait()
    load_off.wait()
    local_stats(core)
    pl.semaphore_wait(barrier, len(masks))

    def remote(src, dst, send, recv, mask):
        return pltpu.make_async_remote_copy(
            src_ref=src, dst_ref=dst, send_sem=send, recv_sem=recv,
            device_id=(me ^ mask,), device_id_type=MESH,
        )

    s1 = [
        remote(h.at[:, sib_cols], x.at[my_rows, :], s1_send.at[i], s1_recv.at[i], SIB)
        for i, (h, x) in enumerate(zip(hbm, xs))
    ]
    for c in s1:
        c.start()

    def pick(first):
        def body(p, carry):
            cols = pl.ds(pl.multiple_of(p * 128, 128), 128)
            low = lax.broadcasted_iota(jnp.int32, (1, 128), 1) < 64
            want_a = jnp.where(low, head(0, 2 * p), head(0, 2 * p + 1))
            want_b = jnp.where(low, lax.rem(head(1, 2 * p), 8), lax.rem(head(1, 2 * p + 1), 8))
            want_c = jnp.where(low, lax.rem(head(2, 2 * p), 8), lax.rem(head(2, 2 * p + 1), 8))

            def ones(want, count):
                return [jnp.where(want == t, 1.0, 0.0).astype(BF16) for t in range(count)]

            hot_a, hot_b, hot_c = ones(want_a, 4), ones(want_b, 8), ones(want_c, 8)

            def mix(tiles, hot):
                out = tiles[0] * hot[0]
                for tile, one in zip(tiles[1:], hot[1:]):
                    out += tile * one
                return out

            for n in (first, first + 1):
                tiles = [xs[n][pl.ds(t * TILE, TILE), cols] for t in range(8)]
                hc[n, 0, :, cols] = mix(tiles, hot_c)
                hb[n, 0, :, cols] = mix(tiles, hot_b)
                for s in range(2):
                    ha[n, s, :, cols] = mix(tiles[4 * s : 4 * s + 4], hot_a)
            return carry

        lax.fori_loop(0, PAIRS, body, 0, unroll=True)

    def send_tiles(half):
        two = pl.ds(2 * half, 2)
        base = 7 * half
        copies = []
        for i, m in enumerate(MASK_C):
            copies.append(remote(hc.at[two, 0], hc.at[two, i + 1], x1_send.at[base + i], x1_recv.at[base + i], m))
        for i, m in enumerate(MASK_B):
            copies.append(remote(hb.at[two, 0], hb.at[two, i + 1], x1_send.at[base + 3 + i], x1_recv.at[base + 3 + i], m))
        copies.append(
            remote(ha.at[two, pl.ds(0, 2)], ha.at[two, pl.ds(2, 2)], x1_send.at[base + 6], x1_recv.at[base + 6], MASK_A[0])
        )
        for c in copies:
            c.start()
        return copies

    s1[0].wait()
    s1[1].wait()
    pick(0)
    kv_copies = send_tiles(0)
    s1[2].wait()
    s1[3].wait()
    pick(2)
    qg_copies = send_tiles(1)
    local_stats(other)

    levels = ((ha, 2, sta, ca, cat, ap, adp), (hb, 1, stb, cb, cbt, bp, bdp), (hc, 1, stc, cc, cct, cp, cdp))

    def all_rows(h, n, cols):
        return h[n, :, :, cols].reshape(4 * TILE, 128)

    def own_rows(h, n, slots, cols):
        return h[n, pl.ds(0, slots), :, cols].reshape(slots * TILE, 128)

    def level_stats(h, slots, st, c, ct, kp, kdp):
        width = slots * TILE

        def body(p, carry):
            cols = pl.ds(pl.multiple_of(p * 128, 128), 128)
            out, kp[p], kdp[p] = stats_of(
                all_rows(h, 0, cols), all_rows(h, 1, cols),
                cat2(own_rows(h, 2, slots, cols)), cat2(own_rows(h, 3, slots, cols)),
            )
            for n, x in enumerate(out):
                for i in range(2):
                    st[n, pl.ds(2 * p + i, 1), pl.ds(0, width)] = x[:, i * width : (i + 1) * width]
            return carry

        lax.fori_loop(0, PAIRS, body, 0, unroll=True)

    kv_copies[6].wait()
    level_stats(*levels[0])
    for c in kv_copies[3:6]:
        c.wait()
    level_stats(*levels[1])
    for c in kv_copies[:3]:
        c.wait()
    level_stats(*levels[2])

    row_id = lax.broadcasted_iota(jnp.int32, (8, ROWS), 0)
    lane_tile = lax.broadcasted_iota(jnp.int32, (8, ROWS), 1) // TILE

    def per_head(f, fill):
        out = jnp.full((8, ROWS), fill, jnp.int32)
        for j in range(6):
            out = jnp.where(row_id == j, f(j), out)
        return out

    tile_a = per_head(lambda j: head(0, j), 0)
    tile_b = per_head(live_b, -1)
    tile_c = per_head(live_c, -1)

    def rep4(x):
        return jnp.concatenate([x] * 4, axis=1)

    lse, delta = [], []
    for s in range(2):
        hits = (lane_tile == tile_a, lane_tile + 4 * s == tile_b, lane_tile + 4 * s == tile_c)
        parts = [tuple(lst[n, s] for n in range(3))]
        for hit, st, start in zip(hits, (sta, stb, stc), (s * TILE, 0, 0)):
            peak, tot, d = (rep4(st[n, :, pl.ds(start, TILE)]) for n in range(3))
            parts.append((jnp.where(hit, peak, -FAR), jnp.where(hit, tot, 0.0), jnp.where(hit, d, 0.0)))
        top = parts[0][0]
        for part in parts[1:]:
            top = jnp.maximum(top, part[0])
        total = jnp.zeros((8, ROWS), F32)
        dsum = jnp.zeros((8, ROWS), F32)
        for peak, tot, d in parts:
            factor = jnp.exp2(peak - top)
            total += tot * factor
            dsum += d * factor
        lse.append(top + jnp.log2(total))
        delta.append(dsum / total)
        ls[s, pl.ds(0, 8), :] = lse[s]
        ls[s, pl.ds(8, 8), :] = delta[s]

    def gather8(values, index, tiles):
        out = jnp.zeros((8, TILE), F32)
        for t in tiles:
            out = jnp.where(index[:, :TILE] == t % 8, values[t // 4 % 2][:, t % 4 * TILE : (t % 4 + 1) * TILE], out)
        return out

    for base, values in ((0, lse), (8, delta)):
        halves = []
        for s in range(2):
            out = jnp.zeros((8, TILE), F32)
            for t in range(4):
                out = jnp.where(tile_a[:, :TILE] == t, values[s][:, t * TILE : (t + 1) * TILE], out)
            halves.append(out)
        ea[0, pl.ds(base, 8), :] = jnp.concatenate(halves, axis=1)
        for e, index in ((eb, tile_b), (ec, tile_c)):
            out = gather8(values, index, range(8))
            if base == 0:
                out = jnp.where(index[:, :TILE] < 0, FAR, out)
            e[0, pl.ds(base, 8), :] = jnp.concatenate([out, out], axis=1)

    x2 = []
    for i, m in enumerate(MASK_C):
        x2.append(remote(ec.at[0], ec.at[i + 1], x2_send.at[i], x2_recv.at[i], m))
    for i, m in enumerate(MASK_B):
        x2.append(remote(eb.at[0], eb.at[i + 1], x2_send.at[3 + i], x2_recv.at[3 + i], m))
    x2.append(remote(ea.at[0], ea.at[1], x2_send.at[6], x2_recv.at[6], MASK_A[0]))
    for c in x2:
        c.start()

    low_row = lax.broadcasted_iota(jnp.int32, (1, 128), 1) < 64

    def head_rows(ref, seg, r):
        return jnp.concatenate([ref[seg, pl.ds(r + i, 1), :] for i in range(2)], axis=1)

    def local_back(n, carry):
        seg, p = n // PAIRS, n % PAIRS
        rows = pl.ds(pl.multiple_of(seg * ROWS, ROWS), ROWS)
        cols = pl.ds(pl.multiple_of(p * 128, 128), 128)
        qc, gc = cat2(xq[rows, cols]), cat2(xg[rows, cols])
        peak = jnp.concatenate([lst[0, seg, pl.ds(2 * p + i, 1), :] for i in range(2)], axis=1)
        pb, ds = probs_of(lp[seg, p], ldp[seg, p], peak, head_rows(ls, seg, 2 * p), head_rows(ls, seg, 8 + 2 * p))
        for i in range(2):
            d = pl.ds(pl.multiple_of(p * 128 + i * 64, 64), 64)
            part = slice(i * ROWS, (i + 1) * ROWS)
            acct[0, d, rows] = dot_nn(xvt[seg, d, :], pb[:, part])
            acct[1, d, rows] = dot_nn(xkt[seg, d, :], ds[:, part])
        acc[0, rows, cols] = dot_nn(ds, qc)
        acc[1, rows, cols] = dot_nn(pb, gc)
        return carry

    def level_query(h, slots, st, ct, kp, kdp, e):
        def body(p, carry):
            cols = pl.ds(pl.multiple_of(p * 128, 128), 128)
            kt, vt = all_rows(h, 0, cols).T, all_rows(h, 1, cols).T

            def pair(r0, r1):
                return jnp.concatenate([r0, r1], axis=1) if slots == 2 else jnp.where(low_row, r0, r1)

            lrow = pair(*(e[0, pl.ds(2 * p + i, 1), :] for i in range(2)))
            drow = pair(*(e[0, pl.ds(8 + 2 * p + i, 1), :] for i in range(2)))
            width = slots * TILE
            peak = jnp.concatenate([st[0, pl.ds(2 * p + i, 1), pl.ds(0, width)] for i in range(2)], axis=1)
            for n, (x, w) in enumerate(zip((vt, kt), probs_of(kp[p], kdp[p], peak, lrow, drow))):
                if slots == 2:
                    for i in range(2):
                        d = pl.ds(pl.multiple_of(p * 128 + i * 64, 64), 64)
                        ct[n, d, :] = dot_nn(x[i * 64 : (i + 1) * 64], w[:, i * 128 : (i + 1) * 128])
                else:
                    y = dot_nn(x, w)
                    for i in range(2):
                        d = pl.ds(pl.multiple_of(p * 128 + i * 64, 64), 64)
                        ct[n, d, :] = dup_lanes(y[i * 64 : (i + 1) * 64], i)
            return carry

        lax.fori_loop(0, PAIRS, body, 0, unroll=True)

    def level_key(h, slots, e, c):
        n = slots * TILE

        def body(p, carry):
            cols = pl.ds(pl.multiple_of(p * 128, 128), 128)
            qq, gg = all_rows(h, 2, cols), all_rows(h, 3, cols)
            kc, vc = cat2(own_rows(h, 0, slots, cols)), cat2(own_rows(h, 1, slots, cols))

            def stat_row(r):
                if slots == 2:
                    return jnp.concatenate([e[0, pl.ds(r, 1), :], e[1, pl.ds(r, 1), :]], axis=1)
                s = [e[i, pl.ds(r, 1), :] for i in range(4)]
                return jnp.concatenate([jnp.where(low_row, s[0], s[1]), jnp.where(low_row, s[2], s[3])], axis=1)

            sc = dot_nt(kc, qq) * SCALE2
            dp = dot_nt(vc, gg)
            pbs, dss = [], []
            for i in range(2):
                part = slice(i * n, (i + 1) * n)
                pr = jnp.exp2(sc[part] - stat_row(2 * p + i))
                dss.append((pr * (dp[part] - stat_row(8 + 2 * p + i)) * SCALE).astype(BF16))
                pbs.append(pr.astype(BF16))
            c[0, :, cols] = sel2(dot_nn(jnp.concatenate(dss, axis=0), qq))
            c[1, :, cols] = sel2(dot_nn(jnp.concatenate(pbs, axis=0), gg))
            return carry

        lax.fori_loop(0, PAIRS, body, 0, unroll=True)

    def finish_query():
        def body(p, carry):
            cols = pl.ds(pl.multiple_of(p * 128, 128), 128)
            first = lax.broadcasted_iota(jnp.int32, (128, 128), 0) < 64
            right = lax.broadcasted_iota(jnp.int32, (128, 128), 1) // 64
            pick_a = jnp.where(first, head(0, 2 * p), head(0, 2 * p + 1)) - right
            pick_b = jnp.where(first, live_b(2 * p), live_b(2 * p + 1)) - right
            pick_c = jnp.where(first, live_c(2 * p), live_c(2 * p + 1)) - right
            for o in range(2):
                a, b, c = cat[o, cols, :], cbt[o, cols, :], cct[o, cols, :]
                for s in range(2):
                    dup = dup_lanes(a, s)
                    for t in range(2):
                        j = 2 * s + t
                        total = acct[o, cols, pl.ds(j * 128, 128)] + jnp.where(pick_a == 2 * t, dup, 0.0)
                        total += jnp.where(pick_b == 2 * j, b, 0.0)
                        total += jnp.where(pick_c == 2 * j, c, 0.0)
                        stage[o, pl.ds(j * 128, 128), cols] = total.astype(BF16).T
            return carry

        lax.fori_loop(0, PAIRS, body, 0, unroll=True)

    def finish_key():
        def body(p, carry):
            cols = pl.ds(pl.multiple_of(p * 128, 128), 128)
            low = low_lanes(TILE)
            pick_a = jnp.where(low, head(0, 2 * p), head(0, 2 * p + 1))
            pick_b = jnp.where(low, live_b(2 * p), live_b(2 * p + 1))
            pick_c = jnp.where(low, live_c(2 * p), live_c(2 * p + 1))
            for o in range(2):
                b, c = cb[o, :, cols], cc[o, :, cols]
                for t in range(8):
                    rows = pl.ds(t * TILE, TILE)
                    a = ca[o, pl.ds(t // 4 * TILE, TILE), cols]
                    total = acc[o, rows, cols] + jnp.where(pick_a == t % 4, a, 0.0)
                    total += jnp.where(pick_b == t, b, 0.0)
                    total += jnp.where(pick_c == t, c, 0.0)
                    stage[2 + o, rows, cols] = total.astype(BF16)
            return carry

        lax.fori_loop(0, PAIRS, body, 0, unroll=True)

    o_refs = (o_att, o_dq, o_dk, o_dv)

    def put(outs):
        copies = []
        for o in outs:
            copies.append(remote(stage.at[o, sib_rows, :], o_refs[o].at[:, my_cols], o_send.at[o], o_recv.at[o], SIB))
        for o in outs:
            copies.append(pltpu.make_async_copy(stage.at[o, my_rows, :], o_refs[o].at[:, my_cols], out_sem.at[o]))
        for c in copies:
            c.start()
        return copies

    es = (ea, eb, ec)
    for (h, slots, st, c, ct, kp, kdp), e in zip(levels, es):
        level_query(h, slots, st, ct, kp, kdp, e)
    lax.fori_loop(0, 2 * PAIRS, local_back, 0, unroll=True)
    finish_query()
    final = put((0, 1))
    waits = ((6, 7), (3, 6), (0, 3))
    for (h, slots, st, c, ct, kp, kdp), e, (lo, hi) in zip(levels, es, waits):
        for i in range(lo, hi):
            qg_copies[i].wait()
            x2[i].wait()
        level_key(h, slots, e, c)
    finish_key()
    final += put((2, 3))
    for c in final:
        c.wait()


def hand_on(*refs):
    for i in range(4):
        refs[4 + i][...] = refs[i][...]


def local(query_rows, key_rows, value_rows, grad_out, head_offset):
    rows = jax.ShapeDtypeStruct((ROWS, 2 * HALF), BF16)
    any_spec = pl.BlockSpec(memory_space=pl.ANY)
    dma = pltpu.SemaphoreType.DMA
    tile4 = pltpu.VMEM((4, 4, TILE, HALF), BF16)
    results = pl.pallas_call(
        kernel,
        out_shape=[rows] * 4,
        in_specs=[any_spec] * 5,
        out_specs=[any_spec] * 4,
        scratch_shapes=[pltpu.VMEM((2 * ROWS, HALF), BF16)] * 4
        + [pltpu.VMEM((2, HALF, ROWS), BF16)] * 2
        + [tile4] * 3
        + [
            pltpu.VMEM((2, 2 * ROWS, HALF), F32),
            pltpu.VMEM((2, HALF, 2 * ROWS), F32),
            pltpu.VMEM((4, 2 * ROWS, HALF), BF16),
            pltpu.VMEM((2, 2 * TILE, HALF), F32),
            pltpu.VMEM((2, TILE, HALF), F32),
            pltpu.VMEM((2, TILE, HALF), F32),
        ]
        + [pltpu.VMEM((2, HALF, 128), F32)] * 3
        + [pltpu.VMEM((2, PAIRS, ROWS, 2 * ROWS), F32)] * 2
        + [pltpu.VMEM((PAIRS, ROWS, ROWS), F32)] * 2
        + [pltpu.VMEM((PAIRS, ROWS, 128), F32)] * 4
        + [
            pltpu.VMEM((3, 2, 8, ROWS), F32),
            pltpu.VMEM((3, 8, 128), F32),
            pltpu.VMEM((3, 8, 128), F32),
            pltpu.VMEM((3, 8, 128), F32),
            pltpu.VMEM((2, 16, ROWS), F32),
            pltpu.VMEM((2, 16, 128), F32),
            pltpu.VMEM((4, 16, 128), F32),
            pltpu.VMEM((4, 16, 128), F32),
            pltpu.SMEM((3, HEADS), jnp.int32), dma(()),
            dma((4,)), dma((4,)), dma((4,)), dma((14,)), dma((14,)), dma((7,)), dma((7,)), dma((4,)), dma((4,)), dma((4,)),
        ],
        compiler_params=pltpu.CompilerParams(
            collective_id=0, has_side_effects=True, vmem_limit_bytes=64 * 1024 * 1024
        ),
        cost_estimate=pl.CostEstimate(flops=2_000_000_000, bytes_accessed=3_200_000, transcendentals=3_000_000),
    )(head_offset, query_rows, key_rows, value_rows, grad_out)
    return pl.pallas_call(
        hand_on,
        out_shape=[rows] * 4,
        in_specs=[pl.BlockSpec(memory_space=pltpu.VMEM)] * 4,
        out_specs=[pl.BlockSpec(memory_space=pltpu.VMEM)] * 4,
    )(*results)


def solution(mesh):
    return jax.shard_map(
        local,
        mesh=mesh,
        in_specs=(P("seq", None), P("seq", None), P("seq", None), P("seq", None), P()),
        out_specs=(P("seq", None), P("seq", None), P("seq", None), P("seq", None)),
        check_vma=False,
    )
```

```python
import jax
import jax.numpy as jnp
from jax import lax
from jax.experimental import pallas as pl
from jax.experimental.pallas import tpu as pltpu
from jax.sharding import PartitionSpec as P

HEADS = 12
HEAD_DIM = 64
TILE = 64
PAIRS = 3
HALF = 384
ROWS = 256
SCALE = HEAD_DIM**-0.5
SCALE2 = SCALE * 1.4426950408889634
FAR = 1e30
MESH = pl.DeviceIdType.MESH
SIB = 1
MASK_A = (2,)
MASK_B = (4, 8, 12)
MASK_C = (64, 128, 192)
F32 = jnp.float32
BF16 = jnp.bfloat16


def dot_nt(a, b):
    return lax.dot_general(a, b, (((1,), (1,)), ((), ())), preferred_element_type=F32)


def dot_nn(a, b):
    return lax.dot_general(a, b, (((1,), (0,)), ((), ())), preferred_element_type=F32)


def dot_tn(a, b):
    return lax.dot_general(a, b, (((0,), (0,)), ((), ())), preferred_element_type=F32)


def low_lanes(rows):
    return lax.broadcasted_iota(jnp.int32, (rows, 128), 1) < 64


def cat2(x):
    low = low_lanes(x.shape[0])
    zero = jnp.zeros_like(x)
    return jnp.concatenate([jnp.where(low, x, zero), jnp.where(low, zero, x)], axis=0)


def sel2(y):
    n = y.shape[0] // 2
    return jnp.where(low_lanes(n), y[:n], y[n:])


def stats_of(kk, vv, qc, gc):
    s = dot_nt(kk, qc) * SCALE2
    m = jnp.max(s, axis=0, keepdims=True)
    p = jnp.exp2(s - m)
    tot = jnp.sum(p, axis=0, keepdims=True)
    dp = dot_nt(vv, gc)
    d = jnp.sum(p * dp, axis=0, keepdims=True)
    return (m, tot, d), p, dp


def probs_of(p, dp, peak, lrow, drow):
    p = p * jnp.exp2(peak - lrow)
    return p.astype(BF16), (p * SCALE * (dp - drow)).astype(BF16)


def dup_lanes(x, upper):
    low = low_lanes(x.shape[0])
    other = pltpu.roll(x, 64, 1)
    return jnp.where(low, other, x) if upper else jnp.where(low, x, other)


def kernel(
    off_hbm, q_hbm, k_hbm, v_hbm, g_hbm,
    o_att, o_dq, o_dk, o_dv,
    xq, xk, xv, xg, xkt, xvt, ha, hb, hc, acc, acct, stage, ca, cb, cc, cat, cbt, cct,
    lp, ldp, ap, adp, bp, bdp, cp, cdp,
    lst, sta, stb, stc, ls, ea, eb, ec,
    off, off_sem, in_sem, s1_send, s1_recv, x1_send, x1_recv, x2_send, x2_recv, out_sem, o_send, o_recv,
):
    me = lax.axis_index("seq")
    core = lax.rem(me, 2)
    other = 1 - core
    chip = me // 2
    masks = (SIB,) + MASK_A + MASK_B + MASK_C
    barrier = pltpu.get_barrier_semaphore()
    for m in masks:
        pl.semaphore_signal(barrier, inc=1, device_id=(me ^ m,), device_id_type=MESH)

    my_cols = pl.ds(pl.multiple_of(core * HALF, 128), HALF)
    sib_cols = pl.ds(pl.multiple_of(other * HALF, 128), HALF)
    my_rows = pl.ds(pl.multiple_of(core * ROWS, ROWS), ROWS)
    sib_rows = pl.ds(pl.multiple_of(other * ROWS, ROWS), ROWS)
    hbm = (k_hbm, v_hbm, q_hbm, g_hbm)
    xs = (xk, xv, xq, xg)
    loads = [
        pltpu.make_async_copy(h.at[:, my_cols], x.at[my_rows, :], in_sem.at[i])
        for i, (h, x) in enumerate(zip(hbm, xs))
    ]
    load_off = pltpu.make_async_copy(off_hbm, off, off_sem)
    for c in loads:
        c.start()
    load_off.start()

    def head(level, j):
        return off[level, core * 6 + j]

    def live_b(j):
        o = head(1, j)
        return jnp.where(lax.rem(chip, 2) == o // 8, lax.rem(o, 8), -1)

    def live_c(j):
        o = head(2, j)
        return jnp.where(lax.rem(chip, 32) == o // 8, lax.rem(o, 8), -1)

    def local_stats(seg):
        rows = pl.ds(pl.multiple_of(seg * ROWS, ROWS), ROWS)

        def body(p, carry):
            cols = pl.ds(pl.multiple_of(p * 128, 128), 128)
            kk, vv = xk[rows, cols], xv[rows, cols]
            out, lp[seg, p], ldp[seg, p] = stats_of(kk, vv, cat2(xq[rows, cols]), cat2(xg[rows, cols]))
            xkt[seg, cols, :] = kk.T
            xvt[seg, cols, :] = vv.T
            for n, x in enumerate(out):
                for i in range(2):
                    lst[n, seg, pl.ds(2 * p + i, 1), :] = x[:, i * ROWS : (i + 1) * ROWS]
            return carry

        lax.fori_loop(0, PAIRS, body, 0, unroll=True)

    zero8 = jnp.zeros((8, ROWS), F32)
    for n in range(3):
        for s in range(2):
            lst[n, s] = zero8
        for st in (sta, stb, stc):
            st[n] = zero8[:, :128]

    pl.semaphore_wait(barrier, len(masks))

    def remote(src, dst, send, recv, mask):
        return pltpu.make_async_remote_copy(
            src_ref=src, dst_ref=dst, send_sem=send, recv_sem=recv,
            device_id=(me ^ mask,), device_id_type=MESH,
        )

    s1 = [
        remote(h.at[:, sib_cols], x.at[my_rows, :], s1_send.at[i], s1_recv.at[i], SIB)
        for i, (h, x) in enumerate(zip(hbm, xs))
    ]
    for c in s1:
        c.start()

    def pick(first):
        def body(p, carry):
            cols = pl.ds(pl.multiple_of(p * 128, 128), 128)
            low = lax.broadcasted_iota(jnp.int32, (1, 128), 1) < 64
            want_a = jnp.where(low, head(0, 2 * p), head(0, 2 * p + 1))
            want_b = jnp.where(low, lax.rem(head(1, 2 * p), 8), lax.rem(head(1, 2 * p + 1), 8))
            want_c = jnp.where(low, lax.rem(head(2, 2 * p), 8), lax.rem(head(2, 2 * p + 1), 8))

            def ones(want, count):
                return [jnp.where(want == t, 1.0, 0.0).astype(BF16) for t in range(count)]

            hot_a, hot_b, hot_c = ones(want_a, 4), ones(want_b, 8), ones(want_c, 8)

            def mix(tiles, hot):
                out = tiles[0] * hot[0]
                for tile, one in zip(tiles[1:], hot[1:]):
                    out += tile * one
                return out

            for n in (first, first + 1):
                tiles = [xs[n][pl.ds(t * TILE, TILE), cols] for t in range(8)]
                hc[n, 0, :, cols] = mix(tiles, hot_c)
                hb[n, 0, :, cols] = mix(tiles, hot_b)
                for s in range(2):
                    ha[n, s, :, cols] = mix(tiles[4 * s : 4 * s + 4], hot_a)
            return carry

        lax.fori_loop(0, PAIRS, body, 0, unroll=True)

    keys, queries = pl.ds(0, 2), pl.ds(2, 2)

    def tiles(h, arrays, src, dst, sem, mask):
        return remote(h.at[arrays, src], h.at[arrays, dst], x1_send.at[sem], x1_recv.at[sem], mask)

    kv_c1 = tiles(hc, keys, 0, 1, 0, 64)
    kv_c3 = tiles(hc, keys, 0, 3, 1, 192)
    kv_b1 = tiles(hb, keys, 0, 1, 2, 4)
    kv_b2 = tiles(hb, keys, 0, 2, 3, 8)
    kv_a = tiles(ha, keys, pl.ds(0, 2), pl.ds(2, 2), 4, 2)
    relay_k = tiles(hc, 0, 3, 2, 5, 64)
    relay_v = tiles(hc, 1, 1, 2, 6, 192)
    relay_b = tiles(hb, keys, 1, 3, 7, 8)
    qg_c1 = tiles(hc, queries, 0, 1, 8, 64)
    qg_c3 = tiles(hc, queries, 0, 3, 9, 192)
    qg_b1 = tiles(hb, queries, 0, 1, 10, 4)
    qg_b2 = tiles(hb, queries, 0, 2, 11, 8)
    qg_a = tiles(ha, queries, pl.ds(0, 2), pl.ds(2, 2), 12, 2)
    relay_q = tiles(hc, 2, 3, 2, 13, 64)
    relay_g = tiles(hc, 3, 1, 2, 14, 192)
    relay_qb = tiles(hb, queries, 1, 3, 15, 8)

    loads[0].wait()
    loads[1].wait()
    load_off.wait()
    s1[0].wait()
    s1[1].wait()
    pick(0)
    for c in (kv_c1, kv_c3, kv_b1, kv_b2):
        c.start()
    s1[2].wait()
    s1[3].wait()
    loads[2].wait()
    loads[3].wait()
    pick(2)
    kv_b1.wait_send()
    kv_b2.wait_send()
    kv_a.start()
    local_stats(core)
    kv_c1.wait_send()
    kv_c3.wait_send()
    for c in (qg_c1, qg_c3, qg_b1, qg_b2):
        c.start()
    kv_b1.wait_recv()
    relay_b.start()
    local_stats(other)
    kv_a.wait_send()
    qg_a.start()

    levels = ((ha, 2, sta, ca, cat, ap, adp), (hb, 1, stb, cb, cbt, bp, bdp), (hc, 1, stc, cc, cct, cp, cdp))

    def all_rows(h, n, cols):
        return h[n, :, :, cols].reshape(4 * TILE, 128)

    def own_rows(h, n, slots, cols):
        return h[n, pl.ds(0, slots), :, cols].reshape(slots * TILE, 128)

    def level_stats(h, slots, st, c, ct, kp, kdp):
        width = slots * TILE

        def body(p, carry):
            cols = pl.ds(pl.multiple_of(p * 128, 128), 128)
            out, kp[p], kdp[p] = stats_of(
                all_rows(h, 0, cols), all_rows(h, 1, cols),
                cat2(own_rows(h, 2, slots, cols)), cat2(own_rows(h, 3, slots, cols)),
            )
            for n, x in enumerate(out):
                for i in range(2):
                    st[n, pl.ds(2 * p + i, 1), pl.ds(0, width)] = x[:, i * width : (i + 1) * width]
            return carry

        lax.fori_loop(0, PAIRS, body, 0, unroll=True)

    kv_c3.wait_recv()
    relay_k.start()
    kv_c1.wait_recv()
    relay_v.start()
    kv_a.wait_recv()
    level_stats(*levels[0])
    kv_b2.wait_recv()
    relay_b.wait()
    level_stats(*levels[1])
    qg_b1.wait()
    relay_qb.start()
    qg_c3.wait()
    relay_q.start()
    qg_c1.wait()
    relay_g.start()
    relay_k.wait()
    relay_v.wait()
    level_stats(*levels[2])

    row_id = lax.broadcasted_iota(jnp.int32, (8, ROWS), 0)
    lane_tile = lax.broadcasted_iota(jnp.int32, (8, ROWS), 1) // TILE

    def per_head(f, fill):
        out = jnp.full((8, ROWS), fill, jnp.int32)
        for j in range(6):
            out = jnp.where(row_id == j, f(j), out)
        return out

    tile_a = per_head(lambda j: head(0, j), 0)
    tile_b = per_head(live_b, -1)
    tile_c = per_head(live_c, -1)

    def rep4(x):
        return jnp.concatenate([x] * 4, axis=1)

    lse, delta = [], []
    for s in range(2):
        hits = (lane_tile == tile_a, lane_tile + 4 * s == tile_b, lane_tile + 4 * s == tile_c)
        parts = [tuple(lst[n, s] for n in range(3))]
        for hit, st, start in zip(hits, (sta, stb, stc), (s * TILE, 0, 0)):
            peak, tot, d = (rep4(st[n, :, pl.ds(start, TILE)]) for n in range(3))
            parts.append((jnp.where(hit, peak, -FAR), jnp.where(hit, tot, 0.0), jnp.where(hit, d, 0.0)))
        top = parts[0][0]
        for part in parts[1:]:
            top = jnp.maximum(top, part[0])
        total = jnp.zeros((8, ROWS), F32)
        dsum = jnp.zeros((8, ROWS), F32)
        for peak, tot, d in parts:
            factor = jnp.exp2(peak - top)
            total += tot * factor
            dsum += d * factor
        lse.append(top + jnp.log2(total))
        delta.append(dsum / total)
        ls[s, pl.ds(0, 8), :] = lse[s]
        ls[s, pl.ds(8, 8), :] = delta[s]

    def gather8(values, index, tiles):
        out = jnp.zeros((8, TILE), F32)
        for t in tiles:
            out = jnp.where(index[:, :TILE] == t % 8, values[t // 4 % 2][:, t % 4 * TILE : (t % 4 + 1) * TILE], out)
        return out

    for base, values in ((0, lse), (8, delta)):
        halves = []
        for s in range(2):
            out = jnp.zeros((8, TILE), F32)
            for t in range(4):
                out = jnp.where(tile_a[:, :TILE] == t, values[s][:, t * TILE : (t + 1) * TILE], out)
            halves.append(out)
        ea[0, pl.ds(base, 8), :] = jnp.concatenate(halves, axis=1)
        for e, index in ((eb, tile_b), (ec, tile_c)):
            out = gather8(values, index, range(8))
            if base == 0:
                out = jnp.where(index[:, :TILE] < 0, FAR, out)
            e[0, pl.ds(base, 8), :] = jnp.concatenate([out, out], axis=1)

    x2 = []
    for i, m in enumerate(MASK_C):
        x2.append(remote(ec.at[0], ec.at[i + 1], x2_send.at[i], x2_recv.at[i], m))
    for i, m in enumerate(MASK_B):
        x2.append(remote(eb.at[0], eb.at[i + 1], x2_send.at[3 + i], x2_recv.at[3 + i], m))
    x2.append(remote(ea.at[0], ea.at[1], x2_send.at[6], x2_recv.at[6], MASK_A[0]))
    for c in x2:
        c.start()

    low_row = lax.broadcasted_iota(jnp.int32, (1, 128), 1) < 64

    def head_rows(ref, seg, r):
        return jnp.concatenate([ref[seg, pl.ds(r + i, 1), :] for i in range(2)], axis=1)

    def local_back(n, carry):
        seg, p = n // PAIRS, n % PAIRS
        rows = pl.ds(pl.multiple_of(seg * ROWS, ROWS), ROWS)
        cols = pl.ds(pl.multiple_of(p * 128, 128), 128)
        qc, gc = cat2(xq[rows, cols]), cat2(xg[rows, cols])
        peak = jnp.concatenate([lst[0, seg, pl.ds(2 * p + i, 1), :] for i in range(2)], axis=1)
        pb, ds = probs_of(lp[seg, p], ldp[seg, p], peak, head_rows(ls, seg, 2 * p), head_rows(ls, seg, 8 + 2 * p))
        for i in range(2):
            d = pl.ds(pl.multiple_of(p * 128 + i * 64, 64), 64)
            part = slice(i * ROWS, (i + 1) * ROWS)
            acct[0, d, rows] = dot_nn(xvt[seg, d, :], pb[:, part])
            acct[1, d, rows] = dot_nn(xkt[seg, d, :], ds[:, part])
        acc[0, rows, cols] = dot_nn(ds, qc)
        acc[1, rows, cols] = dot_nn(pb, gc)
        return carry

    def level_query(h, slots, st, ct, kp, kdp, e):
        def body(p, carry):
            cols = pl.ds(pl.multiple_of(p * 128, 128), 128)
            kt, vt = all_rows(h, 0, cols).T, all_rows(h, 1, cols).T

            def pair(r0, r1):
                return jnp.concatenate([r0, r1], axis=1) if slots == 2 else jnp.where(low_row, r0, r1)

            lrow = pair(*(e[0, pl.ds(2 * p + i, 1), :] for i in range(2)))
            drow = pair(*(e[0, pl.ds(8 + 2 * p + i, 1), :] for i in range(2)))
            width = slots * TILE
            peak = jnp.concatenate([st[0, pl.ds(2 * p + i, 1), pl.ds(0, width)] for i in range(2)], axis=1)
            for n, (x, w) in enumerate(zip((vt, kt), probs_of(kp[p], kdp[p], peak, lrow, drow))):
                if slots == 2:
                    for i in range(2):
                        d = pl.ds(pl.multiple_of(p * 128 + i * 64, 64), 64)
                        ct[n, d, :] = dot_nn(x[i * 64 : (i + 1) * 64], w[:, i * 128 : (i + 1) * 128])
                else:
                    y = dot_nn(x, w)
                    for i in range(2):
                        d = pl.ds(pl.multiple_of(p * 128 + i * 64, 64), 64)
                        ct[n, d, :] = dup_lanes(y[i * 64 : (i + 1) * 64], i)
            return carry

        lax.fori_loop(0, PAIRS, body, 0, unroll=True)

    def level_key(h, slots, e, c):
        n = slots * TILE

        def body(p, carry):
            cols = pl.ds(pl.multiple_of(p * 128, 128), 128)
            qq, gg = all_rows(h, 2, cols), all_rows(h, 3, cols)
            kc, vc = cat2(own_rows(h, 0, slots, cols)), cat2(own_rows(h, 1, slots, cols))

            def stat_row(r):
                if slots == 2:
                    return jnp.concatenate([e[0, pl.ds(r, 1), :], e[1, pl.ds(r, 1), :]], axis=1)
                s = [e[i, pl.ds(r, 1), :] for i in range(4)]
                return jnp.concatenate([jnp.where(low_row, s[0], s[1]), jnp.where(low_row, s[2], s[3])], axis=1)

            sc = dot_nt(kc, qq) * SCALE2
            dp = dot_nt(vc, gg)
            pbs, dss = [], []
            for i in range(2):
                part = slice(i * n, (i + 1) * n)
                pr = jnp.exp2(sc[part] - stat_row(2 * p + i))
                dss.append((pr * (dp[part] - stat_row(8 + 2 * p + i)) * SCALE).astype(BF16))
                pbs.append(pr.astype(BF16))
            c[0, :, cols] = sel2(dot_nn(jnp.concatenate(dss, axis=0), qq))
            c[1, :, cols] = sel2(dot_nn(jnp.concatenate(pbs, axis=0), gg))
            return carry

        lax.fori_loop(0, PAIRS, body, 0, unroll=True)

    def finish_query():
        def body(p, carry):
            cols = pl.ds(pl.multiple_of(p * 128, 128), 128)
            first = lax.broadcasted_iota(jnp.int32, (128, 128), 0) < 64
            right = lax.broadcasted_iota(jnp.int32, (128, 128), 1) // 64
            pick_a = jnp.where(first, head(0, 2 * p), head(0, 2 * p + 1)) - right
            pick_b = jnp.where(first, live_b(2 * p), live_b(2 * p + 1)) - right
            pick_c = jnp.where(first, live_c(2 * p), live_c(2 * p + 1)) - right
            for o in range(2):
                a, b, c = cat[o, cols, :], cbt[o, cols, :], cct[o, cols, :]
                for s in range(2):
                    dup = dup_lanes(a, s)
                    for t in range(2):
                        j = 2 * s + t
                        total = acct[o, cols, pl.ds(j * 128, 128)] + jnp.where(pick_a == 2 * t, dup, 0.0)
                        total += jnp.where(pick_b == 2 * j, b, 0.0)
                        total += jnp.where(pick_c == 2 * j, c, 0.0)
                        stage[o, pl.ds(j * 128, 128), cols] = total.astype(BF16).T
            return carry

        lax.fori_loop(0, PAIRS, body, 0, unroll=True)

    def finish_near():
        def body(p, carry):
            cols = pl.ds(pl.multiple_of(p * 128, 128), 128)
            low = low_lanes(TILE)
            pick_a = jnp.where(low, head(0, 2 * p), head(0, 2 * p + 1))
            pick_b = jnp.where(low, live_b(2 * p), live_b(2 * p + 1))
            for o in range(2):
                b = cb[o, :, cols]
                for t in range(8):
                    rows = pl.ds(t * TILE, TILE)
                    a = ca[o, pl.ds(t // 4 * TILE, TILE), cols]
                    total = acc[o, rows, cols] + jnp.where(pick_a == t % 4, a, 0.0)
                    acc[o, rows, cols] = total + jnp.where(pick_b == t, b, 0.0)
            return carry

        lax.fori_loop(0, PAIRS, body, 0, unroll=True)

    def finish_key():
        def body(p, carry):
            cols = pl.ds(pl.multiple_of(p * 128, 128), 128)
            pick_c = jnp.where(low_lanes(TILE), live_c(2 * p), live_c(2 * p + 1))
            for o in range(2):
                c = cc[o, :, cols]
                for t in range(8):
                    rows = pl.ds(t * TILE, TILE)
                    total = acc[o, rows, cols] + jnp.where(pick_c == t, c, 0.0)
                    stage[2 + o, rows, cols] = total.astype(BF16)
            return carry

        lax.fori_loop(0, PAIRS, body, 0, unroll=True)

    o_refs = (o_att, o_dq, o_dk, o_dv)

    def put(outs):
        copies = []
        for o in outs:
            copies.append(remote(stage.at[o, sib_rows, :], o_refs[o].at[:, my_cols], o_send.at[o], o_recv.at[o], SIB))
        for o in outs:
            copies.append(pltpu.make_async_copy(stage.at[o, my_rows, :], o_refs[o].at[:, my_cols], out_sem.at[o]))
        for c in copies:
            c.start()
        return copies

    es = (ea, eb, ec)
    for (h, slots, st, c, ct, kp, kdp), e in zip(levels, es):
        level_query(h, slots, st, ct, kp, kdp, e)
    lax.fori_loop(0, 2 * PAIRS, local_back, 0, unroll=True)
    finish_query()
    final = put((0, 1))
    x2_of = (x2[6:], x2[3:6], x2[:3])
    for (h, slots, st, c, ct, kp, kdp), e, tile_copies, row_copies in zip(levels, es, ([qg_a], [qg_b2, relay_qb], [relay_q, relay_g]), x2_of):
        if h is hc:
            finish_near()
        for copy in tile_copies + row_copies:
            copy.wait()
        level_key(h, slots, e, c)
    finish_key()
    final += put((2, 3))
    for c in final:
        c.wait()


def hand_on(*refs):
    ins, outs, (held, in_sem, out_sem) = refs[:4], refs[4:8], refs[8:]
    loads = [pltpu.make_async_copy(ins[i], held.at[i], in_sem.at[i]) for i in range(4)]
    stores = [pltpu.make_async_copy(held.at[i], outs[i], out_sem.at[i]) for i in range(4)]
    for c in loads:
        c.start()
    for load, store in zip(loads, stores):
        load.wait()
        store.start()
    for c in stores:
        c.wait()


def local(query_rows, key_rows, value_rows, grad_out, head_offset):
    rows = jax.ShapeDtypeStruct((ROWS, 2 * HALF), BF16)
    any_spec = pl.BlockSpec(memory_space=pl.ANY)
    dma = pltpu.SemaphoreType.DMA
    tile4 = pltpu.VMEM((4, 4, TILE, HALF), BF16)
    results = pl.pallas_call(
        kernel,
        out_shape=[rows] * 4,
        in_specs=[any_spec] * 5,
        out_specs=[any_spec] * 4,
        scratch_shapes=[pltpu.VMEM((2 * ROWS, HALF), BF16)] * 4
        + [pltpu.VMEM((2, HALF, ROWS), BF16)] * 2
        + [tile4] * 3
        + [
            pltpu.VMEM((2, 2 * ROWS, HALF), F32),
            pltpu.VMEM((2, HALF, 2 * ROWS), F32),
            pltpu.VMEM((4, 2 * ROWS, HALF), BF16),
            pltpu.VMEM((2, 2 * TILE, HALF), F32),
            pltpu.VMEM((2, TILE, HALF), F32),
            pltpu.VMEM((2, TILE, HALF), F32),
        ]
        + [pltpu.VMEM((2, HALF, 128), F32)] * 3
        + [pltpu.VMEM((2, PAIRS, ROWS, 2 * ROWS), F32)] * 2
        + [pltpu.VMEM((PAIRS, ROWS, ROWS), F32)] * 2
        + [pltpu.VMEM((PAIRS, ROWS, 128), F32)] * 4
        + [
            pltpu.VMEM((3, 2, 8, ROWS), F32),
            pltpu.VMEM((3, 8, 128), F32),
            pltpu.VMEM((3, 8, 128), F32),
            pltpu.VMEM((3, 8, 128), F32),
            pltpu.VMEM((2, 16, ROWS), F32),
            pltpu.VMEM((2, 16, 128), F32),
            pltpu.VMEM((4, 16, 128), F32),
            pltpu.VMEM((4, 16, 128), F32),
            pltpu.SMEM((3, HEADS), jnp.int32), dma(()),
            dma((4,)), dma((4,)), dma((4,)), dma((16,)), dma((16,)), dma((7,)), dma((7,)), dma((4,)), dma((4,)), dma((4,)),
        ],
        compiler_params=pltpu.CompilerParams(
            collective_id=0, has_side_effects=True, vmem_limit_bytes=64 * 1024 * 1024
        ),
        cost_estimate=pl.CostEstimate(flops=2_000_000_000, bytes_accessed=3_200_000, transcendentals=3_000_000),
    )(head_offset, query_rows, key_rows, value_rows, grad_out)
    return pl.pallas_call(
        hand_on,
        out_shape=[rows] * 4,
        in_specs=[any_spec] * 4,
        out_specs=[any_spec] * 4,
        scratch_shapes=[pltpu.VMEM((4, ROWS, 2 * HALF), BF16), dma((4,)), dma((4,))],
        compiler_params=pltpu.CompilerParams(vmem_limit_bytes=64 * 1024 * 1024),
    )(*results)


def solution(mesh):
    return jax.shard_map(
        local,
        mesh=mesh,
        in_specs=(P("seq", None), P("seq", None), P("seq", None), P("seq", None), P()),
        out_specs=(P("seq", None), P("seq", None), P("seq", None), P("seq", None)),
        check_vma=False,
    )
```

```python
import jax
import jax.numpy as jnp
from jax import lax
from jax.experimental import pallas as pl
from jax.experimental.pallas import tpu as pltpu
from jax.sharding import PartitionSpec as P

HEADS = 12
HEAD_DIM = 64
TILE = 64
PAIRS = 3
HALF = 384
ROWS = 256
SCALE = HEAD_DIM**-0.5
SCALE2 = SCALE * 1.4426950408889634
FAR = 1e30
MESH = pl.DeviceIdType.MESH
SIB = 1
MASK_A = (2,)
MASK_B = (4, 8, 12)
MASK_C = (64, 128, 192)
F32 = jnp.float32
BF16 = jnp.bfloat16


def dot_nt(a, b):
    return lax.dot_general(a, b, (((1,), (1,)), ((), ())), preferred_element_type=F32)


def dot_nn(a, b):
    return lax.dot_general(a, b, (((1,), (0,)), ((), ())), preferred_element_type=F32)


def dot_tn(a, b):
    return lax.dot_general(a, b, (((0,), (0,)), ((), ())), preferred_element_type=F32)


def low_lanes(rows):
    return lax.broadcasted_iota(jnp.int32, (rows, 128), 1) < 64


def cat2(x):
    low = low_lanes(x.shape[0])
    zero = jnp.zeros_like(x)
    return jnp.concatenate([jnp.where(low, x, zero), jnp.where(low, zero, x)], axis=0)


def sel2(y):
    n = y.shape[0] // 2
    return jnp.where(low_lanes(n), y[:n], y[n:])


def stats_of(kk, vv, qc, gc):
    s = dot_nt(kk, qc) * SCALE2
    m = jnp.max(s, axis=0, keepdims=True)
    p = jnp.exp2(s - m)
    tot = jnp.sum(p, axis=0, keepdims=True)
    dp = dot_nt(vv, gc)
    d = jnp.sum(p * dp, axis=0, keepdims=True)
    return (m, tot, d), p, dp


def probs_of(p, dp, peak, lrow, drow):
    p = p * jnp.exp2(peak - lrow)
    return p.astype(BF16), (p * SCALE * (dp - drow)).astype(BF16)


def dup_lanes(x, upper):
    low = low_lanes(x.shape[0])
    other = pltpu.roll(x, 64, 1)
    return jnp.where(low, other, x) if upper else jnp.where(low, x, other)


def kernel(
    off_hbm, q_hbm, k_hbm, v_hbm, g_hbm,
    o_att, o_dq, o_dk, o_dv,
    xq, xk, xv, xg, xkt, xvt, ha, hb, hc, acc, acct, stage, ca, cb, cc, cat, cbt, cct,
    lp, ldp, ap, adp, bp, bdp, cp, cdp,
    lst, sta, stb, stc, ls, ea, eb, ec,
    off, off_sem, in_sem, s1_send, s1_recv, x1_send, x1_recv, x2_send, x2_recv, out_sem, o_send, o_recv,
):
    me = lax.axis_index("seq")
    core = lax.rem(me, 2)
    other = 1 - core
    chip = me // 2
    masks = (SIB,) + MASK_A + MASK_B + MASK_C
    barrier = pltpu.get_barrier_semaphore()
    for m in masks:
        pl.semaphore_signal(barrier, inc=1, device_id=(me ^ m,), device_id_type=MESH)

    my_cols = pl.ds(pl.multiple_of(core * HALF, 128), HALF)
    sib_cols = pl.ds(pl.multiple_of(other * HALF, 128), HALF)
    my_rows = pl.ds(pl.multiple_of(core * ROWS, ROWS), ROWS)
    sib_rows = pl.ds(pl.multiple_of(other * ROWS, ROWS), ROWS)
    hbm = (k_hbm, v_hbm, q_hbm, g_hbm)
    xs = (xk, xv, xq, xg)
    loads = [
        pltpu.make_async_copy(h.at[:, my_cols], x.at[my_rows, :], in_sem.at[i])
        for i, (h, x) in enumerate(zip(hbm, xs))
    ]
    load_off = pltpu.make_async_copy(off_hbm, off, off_sem)
    for c in loads:
        c.start()
    load_off.start()

    def head(level, j):
        return off[level, core * 6 + j]

    def live_b(j):
        o = head(1, j)
        return jnp.where(lax.rem(chip, 2) == o // 8, lax.rem(o, 8), -1)

    def live_c(j):
        o = head(2, j)
        return jnp.where(lax.rem(chip, 32) == o // 8, lax.rem(o, 8), -1)

    def local_stats(seg):
        rows = pl.ds(pl.multiple_of(seg * ROWS, ROWS), ROWS)

        def body(p, carry):
            cols = pl.ds(pl.multiple_of(p * 128, 128), 128)
            kk, vv = xk[rows, cols], xv[rows, cols]
            out, lp[seg, p], ldp[seg, p] = stats_of(kk, vv, cat2(xq[rows, cols]), cat2(xg[rows, cols]))
            xkt[seg, cols, :] = kk.T
            xvt[seg, cols, :] = vv.T
            for n, x in enumerate(out):
                for i in range(2):
                    lst[n, seg, pl.ds(2 * p + i, 1), :] = x[:, i * ROWS : (i + 1) * ROWS]
            return carry

        lax.fori_loop(0, PAIRS, body, 0, unroll=True)

    zero8 = jnp.zeros((8, ROWS), F32)
    for n in range(3):
        for s in range(2):
            lst[n, s] = zero8
        for st in (sta, stb, stc):
            st[n] = zero8[:, :128]

    pl.semaphore_wait(barrier, len(masks))

    def remote(src, dst, send, recv, mask):
        return pltpu.make_async_remote_copy(
            src_ref=src, dst_ref=dst, send_sem=send, recv_sem=recv,
            device_id=(me ^ mask,), device_id_type=MESH,
        )

    s1 = [
        remote(h.at[:, sib_cols], x.at[my_rows, :], s1_send.at[i], s1_recv.at[i], SIB)
        for i, (h, x) in enumerate(zip(hbm, xs))
    ]
    for c in s1:
        c.start()

    def pick(*arrays):
        def body(p, carry):
            cols = pl.ds(pl.multiple_of(p * 128, 128), 128)
            low = lax.broadcasted_iota(jnp.int32, (1, 128), 1) < 64
            want_a = jnp.where(low, head(0, 2 * p), head(0, 2 * p + 1))
            want_b = jnp.where(low, lax.rem(head(1, 2 * p), 8), lax.rem(head(1, 2 * p + 1), 8))
            want_c = jnp.where(low, lax.rem(head(2, 2 * p), 8), lax.rem(head(2, 2 * p + 1), 8))

            def ones(want, count):
                return [jnp.where(want == t, 1.0, 0.0).astype(BF16) for t in range(count)]

            hot_a, hot_b, hot_c = ones(want_a, 4), ones(want_b, 8), ones(want_c, 8)

            def mix(tiles, hot):
                out = tiles[0] * hot[0]
                for tile, one in zip(tiles[1:], hot[1:]):
                    out += tile * one
                return out

            for n in arrays:
                tiles = [xs[n][pl.ds(t * TILE, TILE), cols] for t in range(8)]
                hc[n, 0, :, cols] = mix(tiles, hot_c)
                hb[n, 0, :, cols] = mix(tiles, hot_b)
                for s in range(2):
                    ha[n, s, :, cols] = mix(tiles[4 * s : 4 * s + 4], hot_a)
            return carry

        lax.fori_loop(0, PAIRS, body, 0, unroll=True)

    keys, queries = pl.ds(0, 2), pl.ds(2, 2)

    def tiles(h, arrays, src, dst, sem, mask):
        return remote(h.at[arrays, src], h.at[arrays, dst], x1_send.at[sem], x1_recv.at[sem], mask)

    up = [tiles(hc, n, 0, 1, n, 64) for n in range(4)]
    down = [tiles(hc, n, 0, 3, 4 + n, 192) for n in range(4)]
    relay_k, relay_q = (tiles(hc, n, 3, 2, 8 + n, 64) for n in (0, 2))
    relay_v, relay_g = (tiles(hc, n, 1, 2, 8 + n, 192) for n in (1, 3))
    kv_b1 = tiles(hb, keys, 0, 1, 12, 4)
    kv_b2 = tiles(hb, keys, 0, 2, 13, 8)
    kv_a = tiles(ha, keys, pl.ds(0, 2), pl.ds(2, 2), 14, 2)
    relay_b = tiles(hb, keys, 1, 3, 15, 8)
    qg_b1 = tiles(hb, queries, 0, 1, 16, 4)
    qg_b2 = tiles(hb, queries, 0, 2, 17, 8)
    qg_a = tiles(ha, queries, pl.ds(0, 2), pl.ds(2, 2), 18, 2)
    relay_qb = tiles(hb, queries, 1, 3, 19, 8)

    load_off.wait()
    loads[0].wait()
    s1[0].wait()
    pick(0)
    down[0].start()
    loads[1].wait()
    s1[1].wait()
    pick(1)
    for c in (up[1], kv_b1, kv_b2):
        c.start()
    for c in loads[2:] + s1[2:]:
        c.wait()
    pick(2, 3)
    down[0].wait_send()
    down[1].start()
    up[1].wait_send()
    up[0].start()
    kv_b1.wait_send()
    kv_b2.wait_send()
    kv_a.start()
    local_stats(core)
    down[1].wait_send()
    down[2].start()
    up[0].wait_send()
    up[3].start()
    qg_b1.start()
    qg_b2.start()
    kv_b1.wait_recv()
    relay_b.start()
    down[0].wait_recv()
    relay_k.start()
    up[1].wait_recv()
    relay_v.start()
    local_stats(other)
    kv_a.wait_send()
    qg_a.start()
    down[2].wait_send()
    down[3].start()
    up[3].wait_send()
    up[2].start()

    levels = ((ha, 2, sta, ca, cat, ap, adp), (hb, 1, stb, cb, cbt, bp, bdp), (hc, 1, stc, cc, cct, cp, cdp))

    def all_rows(h, n, cols):
        return h[n, :, :, cols].reshape(4 * TILE, 128)

    def own_rows(h, n, slots, cols):
        return h[n, pl.ds(0, slots), :, cols].reshape(slots * TILE, 128)

    def level_stats(h, slots, st, c, ct, kp, kdp):
        width = slots * TILE

        def body(p, carry):
            cols = pl.ds(pl.multiple_of(p * 128, 128), 128)
            out, kp[p], kdp[p] = stats_of(
                all_rows(h, 0, cols), all_rows(h, 1, cols),
                cat2(own_rows(h, 2, slots, cols)), cat2(own_rows(h, 3, slots, cols)),
            )
            for n, x in enumerate(out):
                for i in range(2):
                    st[n, pl.ds(2 * p + i, 1), pl.ds(0, width)] = x[:, i * width : (i + 1) * width]
            return carry

        lax.fori_loop(0, PAIRS, body, 0, unroll=True)

    kv_a.wait_recv()
    level_stats(*levels[0])
    kv_b2.wait_recv()
    relay_b.wait()
    level_stats(*levels[1])
    down[1].wait_recv()
    up[0].wait_recv()
    relay_k.wait()
    relay_v.wait()
    level_stats(*levels[2])
    qg_b1.wait()
    relay_qb.start()
    down[2].wait_recv()
    relay_q.start()
    up[3].wait_recv()
    relay_g.start()

    row_id = lax.broadcasted_iota(jnp.int32, (8, ROWS), 0)
    lane_tile = lax.broadcasted_iota(jnp.int32, (8, ROWS), 1) // TILE

    def per_head(f, fill):
        out = jnp.full((8, ROWS), fill, jnp.int32)
        for j in range(6):
            out = jnp.where(row_id == j, f(j), out)
        return out

    tile_a = per_head(lambda j: head(0, j), 0)
    tile_b = per_head(live_b, -1)
    tile_c = per_head(live_c, -1)

    def rep4(x):
        return jnp.concatenate([x] * 4, axis=1)

    lse, delta = [], []
    for s in range(2):
        hits = (lane_tile == tile_a, lane_tile + 4 * s == tile_b, lane_tile + 4 * s == tile_c)
        parts = [tuple(lst[n, s] for n in range(3))]
        for hit, st, start in zip(hits, (sta, stb, stc), (s * TILE, 0, 0)):
            peak, tot, d = (rep4(st[n, :, pl.ds(start, TILE)]) for n in range(3))
            parts.append((jnp.where(hit, peak, -FAR), jnp.where(hit, tot, 0.0), jnp.where(hit, d, 0.0)))
        top = parts[0][0]
        for part in parts[1:]:
            top = jnp.maximum(top, part[0])
        total = jnp.zeros((8, ROWS), F32)
        dsum = jnp.zeros((8, ROWS), F32)
        for peak, tot, d in parts:
            factor = jnp.exp2(peak - top)
            total += tot * factor
            dsum += d * factor
        lse.append(top + jnp.log2(total))
        delta.append(dsum / total)
        ls[s, pl.ds(0, 8), :] = lse[s]
        ls[s, pl.ds(8, 8), :] = delta[s]

    def gather8(values, index, tiles):
        out = jnp.zeros((8, TILE), F32)
        for t in tiles:
            out = jnp.where(index[:, :TILE] == t % 8, values[t // 4 % 2][:, t % 4 * TILE : (t % 4 + 1) * TILE], out)
        return out

    for base, values in ((0, lse), (8, delta)):
        halves = []
        for s in range(2):
            out = jnp.zeros((8, TILE), F32)
            for t in range(4):
                out = jnp.where(tile_a[:, :TILE] == t, values[s][:, t * TILE : (t + 1) * TILE], out)
            halves.append(out)
        ea[0, pl.ds(base, 8), :] = jnp.concatenate(halves, axis=1)
        for e, index in ((eb, tile_b), (ec, tile_c)):
            out = gather8(values, index, range(8))
            if base == 0:
                out = jnp.where(index[:, :TILE] < 0, FAR, out)
            e[0, pl.ds(base, 8), :] = jnp.concatenate([out, out], axis=1)

    x2 = []
    for i, m in enumerate(MASK_C):
        x2.append(remote(ec.at[0], ec.at[i + 1], x2_send.at[i], x2_recv.at[i], m))
    for i, m in enumerate(MASK_B):
        x2.append(remote(eb.at[0], eb.at[i + 1], x2_send.at[3 + i], x2_recv.at[3 + i], m))
    x2.append(remote(ea.at[0], ea.at[1], x2_send.at[6], x2_recv.at[6], MASK_A[0]))
    for c in x2:
        c.start()

    low_row = lax.broadcasted_iota(jnp.int32, (1, 128), 1) < 64

    def head_rows(ref, seg, r):
        return jnp.concatenate([ref[seg, pl.ds(r + i, 1), :] for i in range(2)], axis=1)

    def local_back(n, carry):
        seg, p = n // PAIRS, n % PAIRS
        rows = pl.ds(pl.multiple_of(seg * ROWS, ROWS), ROWS)
        cols = pl.ds(pl.multiple_of(p * 128, 128), 128)
        qc, gc = cat2(xq[rows, cols]), cat2(xg[rows, cols])
        peak = jnp.concatenate([lst[0, seg, pl.ds(2 * p + i, 1), :] for i in range(2)], axis=1)
        pb, ds = probs_of(lp[seg, p], ldp[seg, p], peak, head_rows(ls, seg, 2 * p), head_rows(ls, seg, 8 + 2 * p))
        for i in range(2):
            d = pl.ds(pl.multiple_of(p * 128 + i * 64, 64), 64)
            part = slice(i * ROWS, (i + 1) * ROWS)
            acct[0, d, rows] = dot_nn(xvt[seg, d, :], pb[:, part])
            acct[1, d, rows] = dot_nn(xkt[seg, d, :], ds[:, part])
        acc[0, rows, cols] = dot_nn(ds, qc)
        acc[1, rows, cols] = dot_nn(pb, gc)
        return carry

    def level_query(h, slots, st, ct, kp, kdp, e):
        def body(p, carry):
            cols = pl.ds(pl.multiple_of(p * 128, 128), 128)
            kt, vt = all_rows(h, 0, cols).T, all_rows(h, 1, cols).T

            def pair(r0, r1):
                return jnp.concatenate([r0, r1], axis=1) if slots == 2 else jnp.where(low_row, r0, r1)

            lrow = pair(*(e[0, pl.ds(2 * p + i, 1), :] for i in range(2)))
            drow = pair(*(e[0, pl.ds(8 + 2 * p + i, 1), :] for i in range(2)))
            width = slots * TILE
            peak = jnp.concatenate([st[0, pl.ds(2 * p + i, 1), pl.ds(0, width)] for i in range(2)], axis=1)
            for n, (x, w) in enumerate(zip((vt, kt), probs_of(kp[p], kdp[p], peak, lrow, drow))):
                if slots == 2:
                    for i in range(2):
                        d = pl.ds(pl.multiple_of(p * 128 + i * 64, 64), 64)
                        ct[n, d, :] = dot_nn(x[i * 64 : (i + 1) * 64], w[:, i * 128 : (i + 1) * 128])
                else:
                    y = dot_nn(x, w)
                    for i in range(2):
                        d = pl.ds(pl.multiple_of(p * 128 + i * 64, 64), 64)
                        ct[n, d, :] = dup_lanes(y[i * 64 : (i + 1) * 64], i)
            return carry

        lax.fori_loop(0, PAIRS, body, 0, unroll=True)

    def level_key(h, slots, e, c):
        n = slots * TILE

        def body(p, carry):
            cols = pl.ds(pl.multiple_of(p * 128, 128), 128)
            qq, gg = all_rows(h, 2, cols), all_rows(h, 3, cols)
            kc, vc = cat2(own_rows(h, 0, slots, cols)), cat2(own_rows(h, 1, slots, cols))

            def stat_row(r):
                if slots == 2:
                    return jnp.concatenate([e[0, pl.ds(r, 1), :], e[1, pl.ds(r, 1), :]], axis=1)
                s = [e[i, pl.ds(r, 1), :] for i in range(4)]
                return jnp.concatenate([jnp.where(low_row, s[0], s[1]), jnp.where(low_row, s[2], s[3])], axis=1)

            sc = dot_nt(kc, qq) * SCALE2
            dp = dot_nt(vc, gg)
            pbs, dss = [], []
            for i in range(2):
                part = slice(i * n, (i + 1) * n)
                pr = jnp.exp2(sc[part] - stat_row(2 * p + i))
                dss.append((pr * (dp[part] - stat_row(8 + 2 * p + i)) * SCALE).astype(BF16))
                pbs.append(pr.astype(BF16))
            c[0, :, cols] = sel2(dot_nn(jnp.concatenate(dss, axis=0), qq))
            c[1, :, cols] = sel2(dot_nn(jnp.concatenate(pbs, axis=0), gg))
            return carry

        lax.fori_loop(0, PAIRS, body, 0, unroll=True)

    def finish_query():
        def body(p, carry):
            cols = pl.ds(pl.multiple_of(p * 128, 128), 128)
            first = lax.broadcasted_iota(jnp.int32, (128, 128), 0) < 64
            right = lax.broadcasted_iota(jnp.int32, (128, 128), 1) // 64
            pick_a = jnp.where(first, head(0, 2 * p), head(0, 2 * p + 1)) - right
            pick_b = jnp.where(first, live_b(2 * p), live_b(2 * p + 1)) - right
            pick_c = jnp.where(first, live_c(2 * p), live_c(2 * p + 1)) - right
            for o in range(2):
                a, b, c = cat[o, cols, :], cbt[o, cols, :], cct[o, cols, :]
                for s in range(2):
                    dup = dup_lanes(a, s)
                    for t in range(2):
                        j = 2 * s + t
                        total = acct[o, cols, pl.ds(j * 128, 128)] + jnp.where(pick_a == 2 * t, dup, 0.0)
                        total += jnp.where(pick_b == 2 * j, b, 0.0)
                        total += jnp.where(pick_c == 2 * j, c, 0.0)
                        stage[o, pl.ds(j * 128, 128), cols] = total.astype(BF16).T
            return carry

        lax.fori_loop(0, PAIRS, body, 0, unroll=True)

    def finish_near():
        def body(p, carry):
            cols = pl.ds(pl.multiple_of(p * 128, 128), 128)
            low = low_lanes(TILE)
            pick_a = jnp.where(low, head(0, 2 * p), head(0, 2 * p + 1))
            pick_b = jnp.where(low, live_b(2 * p), live_b(2 * p + 1))
            for o in range(2):
                b = cb[o, :, cols]
                for t in range(8):
                    rows = pl.ds(t * TILE, TILE)
                    a = ca[o, pl.ds(t // 4 * TILE, TILE), cols]
                    total = acc[o, rows, cols] + jnp.where(pick_a == t % 4, a, 0.0)
                    acc[o, rows, cols] = total + jnp.where(pick_b == t, b, 0.0)
            return carry

        lax.fori_loop(0, PAIRS, body, 0, unroll=True)

    def finish_key():
        def body(p, carry):
            cols = pl.ds(pl.multiple_of(p * 128, 128), 128)
            pick_c = jnp.where(low_lanes(TILE), live_c(2 * p), live_c(2 * p + 1))
            for o in range(2):
                c = cc[o, :, cols]
                for t in range(8):
                    rows = pl.ds(t * TILE, TILE)
                    total = acc[o, rows, cols] + jnp.where(pick_c == t, c, 0.0)
                    stage[2 + o, rows, cols] = total.astype(BF16)
            return carry

        lax.fori_loop(0, PAIRS, body, 0, unroll=True)

    o_refs = (o_att, o_dq, o_dk, o_dv)

    def put(outs):
        copies = []
        for o in outs:
            copies.append(remote(stage.at[o, sib_rows, :], o_refs[o].at[:, my_cols], o_send.at[o], o_recv.at[o], SIB))
        for o in outs:
            copies.append(pltpu.make_async_copy(stage.at[o, my_rows, :], o_refs[o].at[:, my_cols], out_sem.at[o]))
        for c in copies:
            c.start()
        return copies

    es = (ea, eb, ec)
    for (h, slots, st, c, ct, kp, kdp), e in zip(levels, es):
        level_query(h, slots, st, ct, kp, kdp, e)
    lax.fori_loop(0, 2 * PAIRS, local_back, 0, unroll=True)
    finish_query()
    final = put((0, 1))
    x2_of = (x2[6:], x2[3:6], x2[:3])
    for (h, slots, st, c, ct, kp, kdp), e, tile_copies, row_copies in zip(levels, es, ([qg_a], [qg_b2, relay_qb], [relay_q, relay_g]), x2_of):
        if h is hc:
            finish_near()
        for copy in tile_copies + row_copies:
            copy.wait()
        if h is hc:
            down[3].wait()
            up[2].wait()
        level_key(h, slots, e, c)
    finish_key()
    final += put((2, 3))
    for c in final:
        c.wait()


def hand_on(*refs):
    ins, outs, (held, in_sem, out_sem) = refs[:4], refs[4:8], refs[8:]
    loads = [pltpu.make_async_copy(ins[i], held.at[i], in_sem.at[i]) for i in range(4)]
    stores = [pltpu.make_async_copy(held.at[i], outs[i], out_sem.at[i]) for i in range(4)]
    for c in loads:
        c.start()
    for load, store in zip(loads, stores):
        load.wait()
        store.start()
    for c in stores:
        c.wait()


def local(query_rows, key_rows, value_rows, grad_out, head_offset):
    rows = jax.ShapeDtypeStruct((ROWS, 2 * HALF), BF16)
    any_spec = pl.BlockSpec(memory_space=pl.ANY)
    dma = pltpu.SemaphoreType.DMA
    tile4 = pltpu.VMEM((4, 4, TILE, HALF), BF16)
    results = pl.pallas_call(
        kernel,
        out_shape=[rows] * 4,
        in_specs=[any_spec] * 5,
        out_specs=[any_spec] * 4,
        scratch_shapes=[pltpu.VMEM((2 * ROWS, HALF), BF16)] * 4
        + [pltpu.VMEM((2, HALF, ROWS), BF16)] * 2
        + [tile4] * 3
        + [
            pltpu.VMEM((2, 2 * ROWS, HALF), F32),
            pltpu.VMEM((2, HALF, 2 * ROWS), F32),
            pltpu.VMEM((4, 2 * ROWS, HALF), BF16),
            pltpu.VMEM((2, 2 * TILE, HALF), F32),
            pltpu.VMEM((2, TILE, HALF), F32),
            pltpu.VMEM((2, TILE, HALF), F32),
        ]
        + [pltpu.VMEM((2, HALF, 128), F32)] * 3
        + [pltpu.VMEM((2, PAIRS, ROWS, 2 * ROWS), F32)] * 2
        + [pltpu.VMEM((PAIRS, ROWS, ROWS), F32)] * 2
        + [pltpu.VMEM((PAIRS, ROWS, 128), F32)] * 4
        + [
            pltpu.VMEM((3, 2, 8, ROWS), F32),
            pltpu.VMEM((3, 8, 128), F32),
            pltpu.VMEM((3, 8, 128), F32),
            pltpu.VMEM((3, 8, 128), F32),
            pltpu.VMEM((2, 16, ROWS), F32),
            pltpu.VMEM((2, 16, 128), F32),
            pltpu.VMEM((4, 16, 128), F32),
            pltpu.VMEM((4, 16, 128), F32),
            pltpu.SMEM((3, HEADS), jnp.int32), dma(()),
            dma((4,)), dma((4,)), dma((4,)), dma((20,)), dma((20,)), dma((7,)), dma((7,)), dma((4,)), dma((4,)), dma((4,)),
        ],
        compiler_params=pltpu.CompilerParams(
            collective_id=0, has_side_effects=True, vmem_limit_bytes=64 * 1024 * 1024
        ),
        cost_estimate=pl.CostEstimate(flops=2_000_000_000, bytes_accessed=3_200_000, transcendentals=3_000_000),
    )(head_offset, query_rows, key_rows, value_rows, grad_out)
    return pl.pallas_call(
        hand_on,
        out_shape=[rows] * 4,
        in_specs=[any_spec] * 4,
        out_specs=[any_spec] * 4,
        scratch_shapes=[pltpu.VMEM((4, ROWS, 2 * HALF), BF16), dma((4,)), dma((4,))],
        compiler_params=pltpu.CompilerParams(vmem_limit_bytes=64 * 1024 * 1024),
    )(*results)


def solution(mesh):
    return jax.shard_map(
        local,
        mesh=mesh,
        in_specs=(P("seq", None), P("seq", None), P("seq", None), P("seq", None), P()),
        out_specs=(P("seq", None), P("seq", None), P("seq", None), P("seq", None)),
        check_vma=False,
    )
```

```python
import jax
import jax.numpy as jnp
from jax import lax
from jax.experimental import pallas as pl
from jax.experimental.pallas import tpu as pltpu
from jax.sharding import PartitionSpec as P

HEADS = 12
HEAD_DIM = 64
TILE = 64
PAIRS = 3
HALF = 384
ROWS = 256
SCALE = HEAD_DIM**-0.5
SCALE2 = SCALE * 1.4426950408889634
FAR = 1e30
MESH = pl.DeviceIdType.MESH
SIB = 1
MASK_A = (2,)
MASK_B = (4, 8, 12)
MASK_C = (64, 128, 192)
F32 = jnp.float32
BF16 = jnp.bfloat16


def dot_nt(a, b):
    return lax.dot_general(a, b, (((1,), (1,)), ((), ())), preferred_element_type=F32)


def dot_nn(a, b):
    return lax.dot_general(a, b, (((1,), (0,)), ((), ())), preferred_element_type=F32)


def dot_tn(a, b):
    return lax.dot_general(a, b, (((0,), (0,)), ((), ())), preferred_element_type=F32)


def low_lanes(rows):
    return lax.broadcasted_iota(jnp.int32, (rows, 128), 1) < 64


def cat2(x):
    low = low_lanes(x.shape[0])
    zero = jnp.zeros_like(x)
    return jnp.concatenate([jnp.where(low, x, zero), jnp.where(low, zero, x)], axis=0)


def sel2(y):
    n = y.shape[0] // 2
    return jnp.where(low_lanes(n), y[:n], y[n:])


def stats_of(kk, vv, qc, gc):
    s = dot_nt(kk, qc) * SCALE2
    m = jnp.max(s, axis=0, keepdims=True)
    p = jnp.exp2(s - m)
    tot = jnp.sum(p, axis=0, keepdims=True)
    dp = dot_nt(vv, gc)
    d = jnp.sum(p * dp, axis=0, keepdims=True)
    return (m, tot, d), p, dp


def probs_of(p, dp, peak, lrow, drow):
    p = p * jnp.exp2(peak - lrow)
    return p.astype(BF16), (p * SCALE * (dp - drow)).astype(BF16)


def dup_lanes(x, upper):
    low = low_lanes(x.shape[0])
    other = pltpu.roll(x, 64, 1)
    return jnp.where(low, other, x) if upper else jnp.where(low, x, other)


def kernel(
    off_hbm, q_hbm, k_hbm, v_hbm, g_hbm,
    o_att, o_dq, o_dk, o_dv,
    xq, xk, xv, xg, xkt, xvt, ha, hb, hc, acc, acct, stage, ca, cb, cc, cat, cbt, cct,
    lp, ldp, ap, adp, bp, bdp, cp, cdp,
    lst, sta, stb, stc, ls, ea, eb, ec,
    off, off_sem, in_sem, s1_send, s1_recv, x1_send, x1_recv, x2_send, x2_recv, out_sem, o_send, o_recv,
):
    me = lax.axis_index("seq")
    core = lax.rem(me, 2)
    other = 1 - core
    chip = me // 2
    masks = (SIB,) + MASK_A + MASK_B + MASK_C
    barrier = pltpu.get_barrier_semaphore()
    for m in masks:
        pl.semaphore_signal(barrier, inc=1, device_id=(me ^ m,), device_id_type=MESH)

    my_cols = pl.ds(pl.multiple_of(core * HALF, 128), HALF)
    sib_cols = pl.ds(pl.multiple_of(other * HALF, 128), HALF)
    my_rows = pl.ds(pl.multiple_of(core * ROWS, ROWS), ROWS)
    sib_rows = pl.ds(pl.multiple_of(other * ROWS, ROWS), ROWS)
    hbm = (k_hbm, v_hbm, q_hbm, g_hbm)
    xs = (xk, xv, xq, xg)
    loads = [
        pltpu.make_async_copy(h.at[:, my_cols], x.at[my_rows, :], in_sem.at[i])
        for i, (h, x) in enumerate(zip(hbm, xs))
    ]
    load_off = pltpu.make_async_copy(off_hbm, off, off_sem)
    for c in loads:
        c.start()
    load_off.start()

    def head(level, j):
        return off[level, core * 6 + j]

    def live_b(j):
        o = head(1, j)
        return jnp.where(lax.rem(chip, 2) == o // 8, lax.rem(o, 8), -1)

    def live_c(j):
        o = head(2, j)
        return jnp.where(lax.rem(chip, 32) == o // 8, lax.rem(o, 8), -1)

    def local_stats(seg):
        rows = pl.ds(pl.multiple_of(seg * ROWS, ROWS), ROWS)

        def body(p, carry):
            cols = pl.ds(pl.multiple_of(p * 128, 128), 128)
            kk, vv = xk[rows, cols], xv[rows, cols]
            out, lp[seg, p], ldp[seg, p] = stats_of(kk, vv, cat2(xq[rows, cols]), cat2(xg[rows, cols]))
            xkt[seg, cols, :] = kk.T
            xvt[seg, cols, :] = vv.T
            for n, x in enumerate(out):
                for i in range(2):
                    lst[n, seg, pl.ds(2 * p + i, 1), :] = x[:, i * ROWS : (i + 1) * ROWS]
            return carry

        lax.fori_loop(0, PAIRS, body, 0, unroll=True)

    zero8 = jnp.zeros((8, ROWS), F32)
    for n in range(3):
        for s in range(2):
            lst[n, s] = zero8
        for st in (sta, stb, stc):
            st[n] = zero8[:, :128]

    pl.semaphore_wait(barrier, len(masks))

    def remote(src, dst, send, recv, mask):
        return pltpu.make_async_remote_copy(
            src_ref=src, dst_ref=dst, send_sem=send, recv_sem=recv,
            device_id=(me ^ mask,), device_id_type=MESH,
        )

    s1 = [
        remote(h.at[:, sib_cols], x.at[my_rows, :], s1_send.at[i], s1_recv.at[i], SIB)
        for i, (h, x) in enumerate(zip(hbm, xs))
    ]
    s1[0].start()
    s1[1].start()

    def pick(*arrays):
        def body(p, carry):
            cols = pl.ds(pl.multiple_of(p * 128, 128), 128)
            low = lax.broadcasted_iota(jnp.int32, (1, 128), 1) < 64
            want_a = jnp.where(low, head(0, 2 * p), head(0, 2 * p + 1))
            want_b = jnp.where(low, lax.rem(head(1, 2 * p), 8), lax.rem(head(1, 2 * p + 1), 8))
            want_c = jnp.where(low, lax.rem(head(2, 2 * p), 8), lax.rem(head(2, 2 * p + 1), 8))

            def ones(want, count):
                return [jnp.where(want == t, 1.0, 0.0).astype(BF16) for t in range(count)]

            hot_a, hot_b, hot_c = ones(want_a, 4), ones(want_b, 8), ones(want_c, 8)

            def mix(tiles, hot):
                out = tiles[0] * hot[0]
                for tile, one in zip(tiles[1:], hot[1:]):
                    out += tile * one
                return out

            for n in arrays:
                tiles = [xs[n][pl.ds(t * TILE, TILE), cols] for t in range(8)]
                hc[n, 0, :, cols] = mix(tiles, hot_c)
                hb[n, 0, :, cols] = mix(tiles, hot_b)
                for s in range(2):
                    ha[n, s, :, cols] = mix(tiles[4 * s : 4 * s + 4], hot_a)
            return carry

        lax.fori_loop(0, PAIRS, body, 0, unroll=True)

    keys, queries = pl.ds(0, 2), pl.ds(2, 2)

    def tiles(h, arrays, src, dst, sem, mask):
        return remote(h.at[arrays, src], h.at[arrays, dst], x1_send.at[sem], x1_recv.at[sem], mask)

    up = [tiles(hc, n, 0, 1, n, 64) for n in range(4)]
    down = [tiles(hc, n, 0, 3, 4 + n, 192) for n in range(4)]
    relay_k, relay_q = (tiles(hc, n, 3, 2, 8 + n, 64) for n in (0, 2))
    relay_v, relay_g = (tiles(hc, n, 1, 2, 8 + n, 192) for n in (1, 3))
    kv_b1 = tiles(hb, keys, 0, 1, 12, 4)
    kv_b2 = tiles(hb, keys, 0, 2, 13, 8)
    kv_a = tiles(ha, keys, pl.ds(0, 2), pl.ds(2, 2), 14, 2)
    relay_b = tiles(hb, keys, 1, 3, 15, 8)
    qg_b1 = tiles(hb, queries, 0, 1, 16, 4)
    qg_b2 = tiles(hb, queries, 0, 2, 17, 8)
    qg_a = tiles(ha, queries, pl.ds(0, 2), pl.ds(2, 2), 18, 2)
    relay_qb = tiles(hb, queries, 1, 3, 19, 8)

    load_off.wait()
    loads[0].wait()
    s1[0].wait()
    s1[2].start()
    pick(0)
    down[0].start()
    loads[1].wait()
    s1[1].wait()
    s1[3].start()
    pick(1)
    for c in (up[1], kv_b1, kv_b2):
        c.start()
    for c in loads[2:] + s1[2:]:
        c.wait()
    pick(2, 3)
    down[0].wait_send()
    down[1].start()
    up[1].wait_send()
    up[0].start()
    kv_b1.wait_send()
    kv_b2.wait_send()
    kv_a.start()
    local_stats(core)
    down[1].wait_send()
    down[2].start()
    up[0].wait_send()
    up[3].start()
    qg_b1.start()
    qg_b2.start()
    kv_b1.wait_recv()
    relay_b.start()
    down[0].wait_recv()
    relay_k.start()
    up[1].wait_recv()
    relay_v.start()
    local_stats(other)
    kv_a.wait_send()
    qg_a.start()
    down[2].wait_send()
    down[3].start()
    up[3].wait_send()
    up[2].start()

    levels = ((ha, 2, sta, ca, cat, ap, adp), (hb, 1, stb, cb, cbt, bp, bdp), (hc, 1, stc, cc, cct, cp, cdp))

    def all_rows(h, n, cols):
        return h[n, :, :, cols].reshape(4 * TILE, 128)

    def own_rows(h, n, slots, cols):
        return h[n, pl.ds(0, slots), :, cols].reshape(slots * TILE, 128)

    def level_stats(h, slots, st, c, ct, kp, kdp):
        width = slots * TILE

        def body(p, carry):
            cols = pl.ds(pl.multiple_of(p * 128, 128), 128)
            out, kp[p], kdp[p] = stats_of(
                all_rows(h, 0, cols), all_rows(h, 1, cols),
                cat2(own_rows(h, 2, slots, cols)), cat2(own_rows(h, 3, slots, cols)),
            )
            for n, x in enumerate(out):
                for i in range(2):
                    st[n, pl.ds(2 * p + i, 1), pl.ds(0, width)] = x[:, i * width : (i + 1) * width]
            return carry

        lax.fori_loop(0, PAIRS, body, 0, unroll=True)

    kv_a.wait_recv()
    level_stats(*levels[0])
    kv_b2.wait_recv()
    relay_b.wait()
    level_stats(*levels[1])
    down[1].wait_recv()
    up[0].wait_recv()
    relay_k.wait()
    relay_v.wait()
    level_stats(*levels[2])
    qg_b1.wait()
    relay_qb.start()
    down[2].wait_recv()
    relay_q.start()
    up[3].wait_recv()
    relay_g.start()

    row_id = lax.broadcasted_iota(jnp.int32, (8, ROWS), 0)
    lane_tile = lax.broadcasted_iota(jnp.int32, (8, ROWS), 1) // TILE

    def per_head(f, fill):
        out = jnp.full((8, ROWS), fill, jnp.int32)
        for j in range(6):
            out = jnp.where(row_id == j, f(j), out)
        return out

    tile_a = per_head(lambda j: head(0, j), 0)
    tile_b = per_head(live_b, -1)
    tile_c = per_head(live_c, -1)

    def rep4(x):
        return jnp.concatenate([x] * 4, axis=1)

    lse, delta = [], []
    for s in range(2):
        hits = (lane_tile == tile_a, lane_tile + 4 * s == tile_b, lane_tile + 4 * s == tile_c)
        parts = [tuple(lst[n, s] for n in range(3))]
        for hit, st, start in zip(hits, (sta, stb, stc), (s * TILE, 0, 0)):
            peak, tot, d = (rep4(st[n, :, pl.ds(start, TILE)]) for n in range(3))
            parts.append((jnp.where(hit, peak, -FAR), jnp.where(hit, tot, 0.0), jnp.where(hit, d, 0.0)))
        top = parts[0][0]
        for part in parts[1:]:
            top = jnp.maximum(top, part[0])
        total = jnp.zeros((8, ROWS), F32)
        dsum = jnp.zeros((8, ROWS), F32)
        for peak, tot, d in parts:
            factor = jnp.exp2(peak - top)
            total += tot * factor
            dsum += d * factor
        lse.append(top + jnp.log2(total))
        delta.append(dsum / total)
        ls[s, pl.ds(0, 8), :] = lse[s]
        ls[s, pl.ds(8, 8), :] = delta[s]

    def gather8(values, index, tiles):
        out = jnp.zeros((8, TILE), F32)
        for t in tiles:
            out = jnp.where(index[:, :TILE] == t % 8, values[t // 4 % 2][:, t % 4 * TILE : (t % 4 + 1) * TILE], out)
        return out

    for base, values in ((0, lse), (8, delta)):
        halves = []
        for s in range(2):
            out = jnp.zeros((8, TILE), F32)
            for t in range(4):
                out = jnp.where(tile_a[:, :TILE] == t, values[s][:, t * TILE : (t + 1) * TILE], out)
            halves.append(out)
        ea[0, pl.ds(base, 8), :] = jnp.concatenate(halves, axis=1)
        for e, index in ((eb, tile_b), (ec, tile_c)):
            out = gather8(values, index, range(8))
            if base == 0:
                out = jnp.where(index[:, :TILE] < 0, FAR, out)
            e[0, pl.ds(base, 8), :] = jnp.concatenate([out, out], axis=1)

    x2 = []
    for i, m in enumerate(MASK_C):
        x2.append(remote(ec.at[0], ec.at[i + 1], x2_send.at[i], x2_recv.at[i], m))
    for i, m in enumerate(MASK_B):
        x2.append(remote(eb.at[0], eb.at[i + 1], x2_send.at[3 + i], x2_recv.at[3 + i], m))
    x2.append(remote(ea.at[0], ea.at[1], x2_send.at[6], x2_recv.at[6], MASK_A[0]))
    for c in x2:
        c.start()

    low_row = lax.broadcasted_iota(jnp.int32, (1, 128), 1) < 64

    def head_rows(ref, seg, r):
        return jnp.concatenate([ref[seg, pl.ds(r + i, 1), :] for i in range(2)], axis=1)

    def local_back(n, carry):
        seg, p = n // PAIRS, n % PAIRS
        rows = pl.ds(pl.multiple_of(seg * ROWS, ROWS), ROWS)
        cols = pl.ds(pl.multiple_of(p * 128, 128), 128)
        qc, gc = cat2(xq[rows, cols]), cat2(xg[rows, cols])
        peak = jnp.concatenate([lst[0, seg, pl.ds(2 * p + i, 1), :] for i in range(2)], axis=1)
        pb, ds = probs_of(lp[seg, p], ldp[seg, p], peak, head_rows(ls, seg, 2 * p), head_rows(ls, seg, 8 + 2 * p))
        for i in range(2):
            d = pl.ds(pl.multiple_of(p * 128 + i * 64, 64), 64)
            part = slice(i * ROWS, (i + 1) * ROWS)
            acct[0, d, rows] = dot_nn(xvt[seg, d, :], pb[:, part])
            acct[1, d, rows] = dot_nn(xkt[seg, d, :], ds[:, part])
        acc[0, rows, cols] = dot_nn(ds, qc)
        acc[1, rows, cols] = dot_nn(pb, gc)
        return carry

    def level_query(h, slots, st, ct, kp, kdp, e):
        def body(p, carry):
            cols = pl.ds(pl.multiple_of(p * 128, 128), 128)
            kt, vt = all_rows(h, 0, cols).T, all_rows(h, 1, cols).T

            def pair(r0, r1):
                return jnp.concatenate([r0, r1], axis=1) if slots == 2 else jnp.where(low_row, r0, r1)

            lrow = pair(*(e[0, pl.ds(2 * p + i, 1), :] for i in range(2)))
            drow = pair(*(e[0, pl.ds(8 + 2 * p + i, 1), :] for i in range(2)))
            width = slots * TILE
            peak = jnp.concatenate([st[0, pl.ds(2 * p + i, 1), pl.ds(0, width)] for i in range(2)], axis=1)
            for n, (x, w) in enumerate(zip((vt, kt), probs_of(kp[p], kdp[p], peak, lrow, drow))):
                if slots == 2:
                    for i in range(2):
                        d = pl.ds(pl.multiple_of(p * 128 + i * 64, 64), 64)
                        ct[n, d, :] = dot_nn(x[i * 64 : (i + 1) * 64], w[:, i * 128 : (i + 1) * 128])
                else:
                    y = dot_nn(x, w)
                    for i in range(2):
                        d = pl.ds(pl.multiple_of(p * 128 + i * 64, 64), 64)
                        ct[n, d, :] = dup_lanes(y[i * 64 : (i + 1) * 64], i)
            return carry

        lax.fori_loop(0, PAIRS, body, 0, unroll=True)

    def level_key(h, slots, e, c):
        n = slots * TILE

        def body(p, carry):
            cols = pl.ds(pl.multiple_of(p * 128, 128), 128)
            qq, gg = all_rows(h, 2, cols), all_rows(h, 3, cols)
            kc, vc = cat2(own_rows(h, 0, slots, cols)), cat2(own_rows(h, 1, slots, cols))

            def stat_row(r):
                if slots == 2:
                    return jnp.concatenate([e[0, pl.ds(r, 1), :], e[1, pl.ds(r, 1), :]], axis=1)
                s = [e[i, pl.ds(r, 1), :] for i in range(4)]
                return jnp.concatenate([jnp.where(low_row, s[0], s[1]), jnp.where(low_row, s[2], s[3])], axis=1)

            sc = dot_nt(kc, qq) * SCALE2
            dp = dot_nt(vc, gg)
            pbs, dss = [], []
            for i in range(2):
                part = slice(i * n, (i + 1) * n)
                pr = jnp.exp2(sc[part] - stat_row(2 * p + i))
                dss.append((pr * (dp[part] - stat_row(8 + 2 * p + i)) * SCALE).astype(BF16))
                pbs.append(pr.astype(BF16))
            c[0, :, cols] = sel2(dot_nn(jnp.concatenate(dss, axis=0), qq))
            c[1, :, cols] = sel2(dot_nn(jnp.concatenate(pbs, axis=0), gg))
            return carry

        lax.fori_loop(0, PAIRS, body, 0, unroll=True)

    def finish_query():
        def body(p, carry):
            cols = pl.ds(pl.multiple_of(p * 128, 128), 128)
            first = lax.broadcasted_iota(jnp.int32, (128, 128), 0) < 64
            right = lax.broadcasted_iota(jnp.int32, (128, 128), 1) // 64
            pick_a = jnp.where(first, head(0, 2 * p), head(0, 2 * p + 1)) - right
            pick_b = jnp.where(first, live_b(2 * p), live_b(2 * p + 1)) - right
            pick_c = jnp.where(first, live_c(2 * p), live_c(2 * p + 1)) - right
            for o in range(2):
                a, b, c = cat[o, cols, :], cbt[o, cols, :], cct[o, cols, :]
                for s in range(2):
                    dup = dup_lanes(a, s)
                    for t in range(2):
                        j = 2 * s + t
                        total = acct[o, cols, pl.ds(j * 128, 128)] + jnp.where(pick_a == 2 * t, dup, 0.0)
                        total += jnp.where(pick_b == 2 * j, b, 0.0)
                        total += jnp.where(pick_c == 2 * j, c, 0.0)
                        stage[o, pl.ds(j * 128, 128), cols] = total.astype(BF16).T
            return carry

        lax.fori_loop(0, PAIRS, body, 0, unroll=True)

    def finish_near():
        def body(p, carry):
            cols = pl.ds(pl.multiple_of(p * 128, 128), 128)
            low = low_lanes(TILE)
            pick_a = jnp.where(low, head(0, 2 * p), head(0, 2 * p + 1))
            pick_b = jnp.where(low, live_b(2 * p), live_b(2 * p + 1))
            for o in range(2):
                b = cb[o, :, cols]
                for t in range(8):
                    rows = pl.ds(t * TILE, TILE)
                    a = ca[o, pl.ds(t // 4 * TILE, TILE), cols]
                    total = acc[o, rows, cols] + jnp.where(pick_a == t % 4, a, 0.0)
                    acc[o, rows, cols] = total + jnp.where(pick_b == t, b, 0.0)
            return carry

        lax.fori_loop(0, PAIRS, body, 0, unroll=True)

    def finish_key():
        def body(p, carry):
            cols = pl.ds(pl.multiple_of(p * 128, 128), 128)
            pick_c = jnp.where(low_lanes(TILE), live_c(2 * p), live_c(2 * p + 1))
            for o in range(2):
                c = cc[o, :, cols]
                for t in range(8):
                    rows = pl.ds(t * TILE, TILE)
                    total = acc[o, rows, cols] + jnp.where(pick_c == t, c, 0.0)
                    stage[2 + o, rows, cols] = total.astype(BF16)
            return carry

        lax.fori_loop(0, PAIRS, body, 0, unroll=True)

    o_refs = (o_att, o_dq, o_dk, o_dv)

    def put(outs):
        copies = []
        for o in outs:
            copies.append(remote(stage.at[o, sib_rows, :], o_refs[o].at[:, my_cols], o_send.at[o], o_recv.at[o], SIB))
        for o in outs:
            copies.append(pltpu.make_async_copy(stage.at[o, my_rows, :], o_refs[o].at[:, my_cols], out_sem.at[o]))
        for c in copies:
            c.start()
        return copies

    es = (ea, eb, ec)
    for (h, slots, st, c, ct, kp, kdp), e in zip(levels, es):
        level_query(h, slots, st, ct, kp, kdp, e)
    lax.fori_loop(0, 2 * PAIRS, local_back, 0, unroll=True)
    finish_query()
    final = put((0, 1))
    x2_of = (x2[6:], x2[3:6], x2[:3])
    for (h, slots, st, c, ct, kp, kdp), e, tile_copies, row_copies in zip(levels, es, ([qg_a], [qg_b2, relay_qb], [relay_q, relay_g]), x2_of):
        if h is hc:
            finish_near()
        for copy in tile_copies + row_copies:
            copy.wait()
        if h is hc:
            down[3].wait()
            up[2].wait()
        level_key(h, slots, e, c)
    finish_key()
    final += put((2, 3))
    for c in final:
        c.wait()


def hand_on(*refs):
    ins, outs, (held, in_sem, out_sem) = refs[:4], refs[4:8], refs[8:]
    loads = [pltpu.make_async_copy(ins[i], held.at[i], in_sem.at[i]) for i in range(4)]
    stores = [pltpu.make_async_copy(held.at[i], outs[i], out_sem.at[i]) for i in range(4)]
    for c in loads:
        c.start()
    for load, store in zip(loads, stores):
        load.wait()
        store.start()
    for c in stores:
        c.wait()


def local(query_rows, key_rows, value_rows, grad_out, head_offset):
    rows = jax.ShapeDtypeStruct((ROWS, 2 * HALF), BF16)
    any_spec = pl.BlockSpec(memory_space=pl.ANY)
    dma = pltpu.SemaphoreType.DMA
    tile4 = pltpu.VMEM((4, 4, TILE, HALF), BF16)
    results = pl.pallas_call(
        kernel,
        out_shape=[rows] * 4,
        in_specs=[any_spec] * 5,
        out_specs=[any_spec] * 4,
        scratch_shapes=[pltpu.VMEM((2 * ROWS, HALF), BF16)] * 4
        + [pltpu.VMEM((2, HALF, ROWS), BF16)] * 2
        + [tile4] * 3
        + [
            pltpu.VMEM((2, 2 * ROWS, HALF), F32),
            pltpu.VMEM((2, HALF, 2 * ROWS), F32),
            pltpu.VMEM((4, 2 * ROWS, HALF), BF16),
            pltpu.VMEM((2, 2 * TILE, HALF), F32),
            pltpu.VMEM((2, TILE, HALF), F32),
            pltpu.VMEM((2, TILE, HALF), F32),
        ]
        + [pltpu.VMEM((2, HALF, 128), F32)] * 3
        + [pltpu.VMEM((2, PAIRS, ROWS, 2 * ROWS), F32)] * 2
        + [pltpu.VMEM((PAIRS, ROWS, ROWS), F32)] * 2
        + [pltpu.VMEM((PAIRS, ROWS, 128), F32)] * 4
        + [
            pltpu.VMEM((3, 2, 8, ROWS), F32),
            pltpu.VMEM((3, 8, 128), F32),
            pltpu.VMEM((3, 8, 128), F32),
            pltpu.VMEM((3, 8, 128), F32),
            pltpu.VMEM((2, 16, ROWS), F32),
            pltpu.VMEM((2, 16, 128), F32),
            pltpu.VMEM((4, 16, 128), F32),
            pltpu.VMEM((4, 16, 128), F32),
            pltpu.SMEM((3, HEADS), jnp.int32), dma(()),
            dma((4,)), dma((4,)), dma((4,)), dma((20,)), dma((20,)), dma((7,)), dma((7,)), dma((4,)), dma((4,)), dma((4,)),
        ],
        compiler_params=pltpu.CompilerParams(
            collective_id=0, has_side_effects=True, vmem_limit_bytes=64 * 1024 * 1024
        ),
        cost_estimate=pl.CostEstimate(flops=2_000_000_000, bytes_accessed=3_200_000, transcendentals=3_000_000),
    )(head_offset, query_rows, key_rows, value_rows, grad_out)
    return pl.pallas_call(
        hand_on,
        out_shape=[rows] * 4,
        in_specs=[any_spec] * 4,
        out_specs=[any_spec] * 4,
        scratch_shapes=[pltpu.VMEM((4, ROWS, 2 * HALF), BF16), dma((4,)), dma((4,))],
        compiler_params=pltpu.CompilerParams(vmem_limit_bytes=64 * 1024 * 1024),
    )(*results)


def solution(mesh):
    return jax.shard_map(
        local,
        mesh=mesh,
        in_specs=(P("seq", None), P("seq", None), P("seq", None), P("seq", None), P()),
        out_specs=(P("seq", None), P("seq", None), P("seq", None), P("seq", None)),
        check_vma=False,
    )
```
